128 devices in a mesh: seq: 32 (over z, y, core), head: 4 (over x).
Axes of the slice: x: 4, y: 4, z: 4, core: 2. Of those that a mesh axis runs over, the one named last changes fastest.
Arguments:
- tokens_x: float32 [32768, 4096], P('seq', 'head'), may hold values from -0.06 to 0.06
- keys: float32 [32768, 32, 128], P('seq', 'head'), may hold values from -0.09375 to 0.09375
- values: float32 [32768, 32, 128], P('seq', 'head'), may hold values from -0.5 to 0.5
- grad_out: float32 [32768, 32, 128], P('seq', 'head'), may hold values from -6 to 6
- level_table: float32 [32, 16, 17], P('head'), may hold values from 0.05 to 1
- level_bins: int32 [32768, 32], P('seq', 'head'), may hold values from 0 to 15
Outputs:
- grad_query: float32 [32768, 32, 128], P('seq', 'head')
- grad_wq: float32 [4096, 4096], P('seq', 'head')
The draws below stay inside these ranges and needn't reach their ends.
All inputs are finite; a program needn't handle non-finite values.
Results may differ from the reference program's by a relative error of at most 0.00011.
Values sent between devices are 32-bit elements; how exact they have to be, the bound alone decides.
A program may use at most 192 MiB of HBM per device.

```python
import math
import jax
import jax.numpy as jnp
import numpy as np
from jax import lax

D = 4096
HEADS = 32
HD = 128
LEVELS = 17
NBINS = 16
TOK_DEV = 1024
TOKENS = 32768
N_SEQ = 32


def place_ends(values, own_key, smallest, high):
    dims = values.shape
    index_at = [jax.random.randint(jax.random.fold_in(own_key, axis), (), 0, dims[axis]) for axis in range(len(dims))]
    values = values.at[tuple(index_at)].set(smallest)
    longest = dims.index(max(dims))
    index_at[longest] = (index_at[longest] + 1) % dims[longest]
    return values.at[tuple(index_at)].set(high)


def strengthened(values, rng, source, target, parts, factor):
    owner, partner = [(jnp.arange(values.shape[dim]) // (values.shape[dim] // parts)).reshape([-1 if axis == dim else 1 for axis in range(values.ndim)]) for dim in (source, target)]
    chosen = jax.random.permutation(rng, parts)[partner]
    strong = (owner == chosen) | (owner == (partner + parts // 2) % parts)
    return jnp.where(strong, factor * values, values)


def level_of(key, extent, cuts, low, top_value):
    def one(axis_at, blocks):
        steps = jax.random.uniform(jax.random.fold_in(jax.random.fold_in(key, 6), axis_at), (blocks,), jnp.float32, low / len(cuts), top_value / len(cuts))
        return jnp.repeat(jnp.exp(steps), extent[axis_at] // blocks).reshape((-1,) + (1,) * (len(extent) - axis_at - 1))

    loudness = one(*cuts[0])
    for cut in cuts[1:]:
        loudness = loudness * one(*cut)
    return loudness


def normal_values(key, dims, deviation, most, split=(), kind=jnp.bfloat16):
    values = jax.random.normal(key, dims, jnp.float32) * deviation
    if len(split) > 0:
        values = level_of(key, dims, split, -0.22, 0.18) * values
    return jnp.clip(values, min=-most, max=most).astype(kind)


def gaussian_with(rng, dims, scale, most, shards, heavy, kind=jnp.bfloat16):
    array = scale * jax.random.normal(rng, dims, jnp.float32)
    if shards:
        array = array * level_of(rng, dims, shards, -0.22, 0.18)
    return jnp.clip(strengthened(array, jax.random.fold_in(rng, 3), *heavy), -most, most).astype(kind)


def setup_inputs(seed: int = 0) -> dict:
    arg_keys = jax.random.split(jax.random.key(seed), 7)
    tokens_x = gaussian_with(arg_keys[0], (TOKENS, D), 0.01, 0.06, ((0, 32), (1, 4)), (0, 1, 32, 2.75), jnp.float32)
    keys = normal_values(arg_keys[1], (TOKENS, HEADS, HD), 0.015625, 0.09375, ((0, 32), (1, 4)), jnp.float32)
    values = normal_values(arg_keys[2], (TOKENS, HEADS, HD), HD ** -0.5, 0.5, ((0, 32), (1, 4)), jnp.float32)
    grad_out = normal_values(arg_keys[3], (TOKENS, HEADS, HD), 1.0, 6.0, ((0, 32), (1, 4)), jnp.float32)
    level_table = jnp.clip(jnp.exp(math.log(1.0) - 2.9957323 * jax.random.uniform(arg_keys[4], (HEADS, NBINS, LEVELS), jnp.float32) ** level_of(arg_keys[4], (HEADS, NBINS, LEVELS), ((0, 4),), -0.2, 0.2)), 0.05, 1.0)
    level_bins = place_ends(jax.random.randint(arg_keys[5], (TOKENS, HEADS), 0, NBINS), jax.random.fold_in(arg_keys[5], 1), 0, NBINS - 1).astype(jnp.int32)
    return {"tokens_x": tokens_x, "keys": keys, "values": values, "grad_out": grad_out, "level_table": level_table, "level_bins": level_bins}


HIGH = lax.Precision.HIGHEST


def level_map(count):
    later = np.arange(count)[:, None]
    earlier = np.arange(count)[None, :]
    differ = later ^ earlier
    result = np.zeros((count, count), np.int64)
    for place in range(24):
        result = result + ((differ >> place) > 0)
    return np.where(earlier <= later, result, -1).astype(np.int32)


def reference(tokens_x, keys, values, grad_out, level_table, level_bins):
    blocks = N_SEQ
    width = TOK_DEV
    span_bits = width.bit_length() - 1
    seq_bits = blocks.bit_length() - 1
    head_ids = jnp.arange(HEADS, dtype=jnp.int32)[None, :]
    weight = level_table[head_ids, level_bins]
    key_blk = keys.reshape(blocks, width, HEADS, HD)
    val_blk = values.reshape(blocks, width, HEADS, HD)
    grad_blk = grad_out.reshape(blocks, width, HEADS, HD)
    weight_blk = weight.reshape(blocks, width, HEADS, LEVELS)
    levels = jnp.asarray(level_map(width))

    def inner(pieces):
        key_piece, val_piece, grad_piece, weight_piece = pieces
        scores = jnp.einsum("thd,shd->hts", grad_piece, val_piece, precision=HIGH)
        mixing = jnp.zeros_like(scores)
        for level in range(span_bits + 1):
            column = jnp.transpose(weight_piece[:, :, level])[:, :, None]
            mixing = mixing + jnp.where((levels == level)[None, :, :], column, 0.0)
        return jnp.einsum("hts,shd->thd", scores * mixing, key_piece, precision=HIGH)

    grad_query = lax.map(inner, (key_blk, val_blk, grad_blk, weight_blk))
    states = jnp.einsum("cthd,cthe->chde", key_blk, val_blk, precision=HIGH)
    block_ids = jnp.arange(blocks, dtype=jnp.int32)
    for place in range(seq_bits):
        sums = states.reshape(blocks >> place, 1 << place, HEADS, HD, HD).sum(axis=1)
        pick = ((block_ids >> place) ^ 1).astype(jnp.int32)
        bucket = sums[pick]
        is_set = ((block_ids >> place) & 1).astype(jnp.float32)
        reading = jnp.einsum("chde,cthe->cthd", bucket, grad_blk, precision=HIGH)
        factor = weight_blk[:, :, :, span_bits + 1 + place][..., None]
        grad_query = grad_query + is_set[:, None, None, None] * factor * reading
    flat = grad_query.reshape(blocks * width, HEADS * HD)
    grad_wq = jnp.einsum("tc,tf->cf", tokens_x, flat, precision=HIGH)
    return grad_query.reshape(blocks * width, HEADS, HD), grad_wq
```

```python
import jax
import jax.numpy as jnp
from jax import lax
from jax.experimental import pallas as pl
from jax.experimental.pallas import tpu as pltpu
from jax.sharding import PartitionSpec as P

MESH = pl.DeviceIdType.MESH
F32 = jnp.float32
BF16 = jnp.bfloat16
NT = (((1,), (1,)), ((), ()))
NN = (((1,), (0,)), ((), ()))


def split(a):
    high = a.astype(BF16)
    return high, (a - high.astype(F32)).astype(BF16)


def mm(a, b, dims=NN):
    return lax.dot_general(a, b, dims, preferred_element_type=F32)


def kernel(
    x_hbm, k_hbm, v_hbm, g_hbm, tab_ref, bins_ref,
    gq_hbm, wq_ref,
    xbuf, kv, gbuf, oq, gt_hi, gt_lo, wts, lev, chunk_st, state, bucket,
    core_in, y_in, z_in, x_hi, x_lo,
    load_sem, out_sem, own_sem, xs, xr, bs, br, ss, sr, cs, cr, ys, yr, zs, zr,
):
    tokens, width = x_hbm.shape
    heads = tab_ref.shape[0]
    hd = 128
    feats = heads * hd
    quarter = tokens // 4
    half_t = tokens // 2
    half_f = feats // 2
    half_h = heads // 2
    span_bits = tokens.bit_length() - 1
    tile = min(256, feats)

    seq = lax.axis_index("seq")
    h = lax.axis_index("head")
    z, y, core = seq // 8, (seq // 2) % 4, seq % 2

    def at(zz, yy, cc):
        return zz * 8 + yy * 2 + cc

    y_up, y_down = (y + 1) % 4, (y + 3) % 4
    z_up, z_down = (z + 1) % 4, (z + 3) % 4
    h_up, h_down = (h + 1) % 4, (h + 3) % 4
    mate = (at(z, y, 1 - core), h)
    to_y_up, to_y_down = (at(z, y_up, core), h), (at(z, y_down, core), h)
    to_z_up, to_z_down = (at(z_up, y, core), h), (at(z_down, y, core), h)
    to_h_up, to_h_down = (seq, h_up), (seq, h_down)
    y_flip = y + 1 - 2 * (y % 2)
    z_flip = z + 1 - 2 * (z % 2)
    y_far, z_far = (y + 2) % 4, (z + 2) % 4
    flips = [
        mate,
        (at(z, y_flip, core), h),
        (at(z, y_far, core), h),
        (at(z_flip, y, core), h),
        (at(z_far, y, core), h),
    ]
    friends = [
        mate, to_y_up, to_y_down, to_z_up, to_z_down, to_h_up, to_h_down, flips[2], flips[4],
    ]

    def rcopy(src, dst, ssem, rsem, dev):
        return pltpu.make_async_remote_copy(
            src_ref=src, dst_ref=dst, send_sem=ssem, recv_sem=rsem,
            device_id=dev, device_id_type=MESH,
        )

    loads = [
        pltpu.make_async_copy(v_hbm, kv.at[pl.ds(tokens * heads, tokens * heads)], load_sem.at[0]),
        pltpu.make_async_copy(k_hbm, kv.at[pl.ds(0, tokens * heads)], load_sem.at[1]),
        pltpu.make_async_copy(g_hbm, gbuf.at[pl.ds(0, tokens * heads)], load_sem.at[2]),
    ]
    for c in loads:
        c.start()

    barrier = pltpu.get_barrier_semaphore()
    for f in friends:
        pl.semaphore_signal(barrier, inc=1, device_id=f, device_id_type=MESH)
    pl.semaphore_wait(barrier, len(friends))

    offsets = (2, 1, 3, 0)

    def x_cols(j):
        yt = (y + offsets[j]) % 4
        return x_hbm.at[:, pl.ds(pl.multiple_of(yt * 256, 256), 256)]

    def x_own(j):
        return pltpu.make_async_copy(x_cols(j), xbuf.at[j], own_sem.at[j])

    def x_right(j):
        return rcopy(x_cols(j), xbuf.at[4 + 2 * j], xs.at[0, j], xr.at[0, j], to_h_up)

    def x_left(j):
        return rcopy(x_cols(j), xbuf.at[5 + 2 * j], xs.at[1, j], xr.at[1, j], to_h_down)

    low_t, high_t = pl.ds(0, half_t), pl.ds(half_t, half_t)

    def x_right2(j):
        return rcopy(
            xbuf.at[4 + 2 * j, low_t], xbuf.at[12 + j, low_t], xs.at[2, j], xr.at[2, j], to_h_up)

    def x_left2(j):
        return rcopy(
            xbuf.at[5 + 2 * j, high_t], xbuf.at[12 + j, high_t], xs.at[3, j], xr.at[3, j], to_h_down)

    for j in range(4):
        x_right(j).start()
        x_left(j).start()
    for j in range(4):
        x_own(j).start()

    loads[0].wait()
    loads[1].wait()

    def head_rows(hh, first=0):
        return pl.ds(first + hh, tokens, stride=heads)

    def states_of(hh, carry):
        kh = kv[head_rows(hh), :]
        vh = kv[head_rows(hh, tokens * heads), :]
        total = None
        for c in range(4):
            rows = slice(c * quarter, (c + 1) * quarter)
            k_hi, k_lo = split(kh[rows])
            v_hi, v_lo = split(vh[rows].T)
            both = mm(v_hi, jnp.concatenate([k_hi, k_lo], axis=1))
            st = both[:, :hd] + both[:, hd:] + mm(v_lo, k_hi)
            chunk_st[hh, c] = st
            total = st if total is None else total + st
        state[hh] = total
        return carry

    lax.fori_loop(0, heads, states_of, 0)

    mine_h = pl.ds(core * half_h, half_h)
    other_h = pl.ds((1 - core) * half_h, half_h)

    def climb(p):
        if p == 0:
            return rcopy(state, bucket.at[0], bs.at[0], br.at[0], mate)
        return rcopy(state.at[mine_h], bucket.at[p, mine_h], bs.at[p], br.at[p], flips[p])

    def share(p):
        return rcopy(bucket.at[p, mine_h], bucket.at[p, mine_h], ss.at[p], sr.at[p], mate)

    def share_in(p):
        return rcopy(bucket.at[p, other_h], bucket.at[p, other_h], ss.at[p], sr.at[p], mate)

    def pump(p):
        climb(p).wait_recv()
        if p > 0:
            share(p).start()
            share_in(p).wait_recv()
        climb(p).wait_send()
        if p < 4:
            state[...] = state[...] + bucket[p]
            climb(p + 1).start()

    climb(0).start()

    for hh in range(heads):
        row = bins_ref[hh:hh + 1, :]
        tab = tab_ref[hh]
        acc = jnp.zeros((tab.shape[0], tokens), F32)
        for b in range(tab.shape[1]):
            acc = acc + jnp.where(row == b, tab[:, b:b + 1], 0.0)
        wts[hh] = acc

    later = lax.broadcasted_iota(jnp.int32, (quarter, quarter), 0)
    earlier = lax.broadcasted_iota(jnp.int32, (quarter, quarter), 1)
    differ = later ^ earlier
    digits = jnp.zeros((quarter, quarter), jnp.int32)
    for place in range(span_bits - 2):
        digits = digits + jnp.where(differ >= (1 << place), 1, 0)
    lev[...] = jnp.where(earlier <= later, digits, -1)

    loads[2].wait()

    def local_of(hh, carry):
        kh = kv[head_rows(hh), :]
        vh = kv[head_rows(hh, tokens * heads), :]
        gh = gbuf[head_rows(hh), :]
        levels = lev[...]
        parts = []
        for c in range(4):
            rows = slice(c * quarter, (c + 1) * quarter)
            k_hi, k_lo = split(kh[rows])
            v_hi, v_lo = split(vh[rows])
            g_hi, g_lo = split(gh[rows])
            g_two = jnp.concatenate([g_hi, g_lo], axis=1)
            scores = mm(g_two, jnp.concatenate([v_hi, v_hi], axis=1), NT) + mm(g_hi, v_lo, NT)
            w = wts[hh, :, rows].T
            mix = jnp.zeros((quarter, quarter), F32)
            for level in range(span_bits - 1):
                mix = jnp.where(levels == level, w[:, level:level + 1], mix)
            m_hi, m_lo = split(scores * mix)
            both = mm(m_hi, jnp.concatenate([k_hi, k_lo], axis=1))
            out = both[:, :hd] + both[:, hd:] + mm(m_lo, k_hi)

            def read(st):
                s_hi, s_lo = split(st)
                return mm(g_two, jnp.concatenate([s_hi, s_hi], axis=0)) + mm(g_hi, s_lo)

            if c % 2:
                out = out + w[:, span_bits - 1:span_bits] * read(chunk_st[hh, c - 1])
            if c >= 2:
                out = out + w[:, span_bits:span_bits + 1] * read(chunk_st[hh, 0] + chunk_st[hh, 1])
            parts.append(out)
        oq[head_rows(hh), :] = jnp.concatenate(parts, axis=0)

        @pl.when(hh == heads // 4 - 1)
        def _():
            pump(0)

        @pl.when(hh == heads - 2)
        def _():
            pump(1)

        return carry

    if heads >= 4:
        lax.fori_loop(0, heads, local_of, 0)
    else:
        for hh in range(heads):
            local_of(hh, 0)
        pump(0)
        pump(1)

    bits = [core, y % 2, y // 2, z % 2, z // 2]

    def read_pair(p):
        on_a = jnp.where(bits[p] == 1, 1.0, 0.0).astype(F32)
        on_b = jnp.where(bits[p + 1] == 1, 1.0, 0.0).astype(F32)
        first = span_bits + 1 + p

        def step(hh, carry):
            g_hi, g_lo = split(gbuf[head_rows(hh), :])
            g_two = jnp.concatenate([g_hi, g_lo], axis=1)
            s_hi, s_lo = split(jnp.concatenate([bucket[p, hh] * on_a, bucket[p + 1, hh] * on_b], axis=1))
            got = mm(g_two, jnp.concatenate([s_hi, s_hi], axis=0)) + mm(g_hi, s_lo)
            w = wts[hh].T
            oq[head_rows(hh), :] = (
                oq[head_rows(hh), :]
                + w[:, first:first + 1] * got[:, :hd]
                + w[:, first + 1:first + 2] * got[:, hd:]
            )
            return carry

        lax.fori_loop(0, heads, step, 0)

    pump(2)
    read_pair(0)
    pump(3)
    read_pair(2)
    pump(4)

    on_last = jnp.where(bits[4] == 1, 1.0, 0.0).astype(F32)

    def finish_head(hh, carry):
        g_hi, g_lo = split(gbuf[head_rows(hh), :])
        g_two = jnp.concatenate([g_hi, g_lo], axis=1)
        s_hi, s_lo = split(bucket[4, hh] * on_last)
        got = mm(g_two, jnp.concatenate([s_hi, s_hi], axis=0)) + mm(g_hi, s_lo)
        last = span_bits + 5
        done = oq[head_rows(hh), :] + wts[hh].T[:, last:last + 1] * got
        oq[head_rows(hh), :] = done
        t_hi, t_lo = split(done.T)
        here = pl.ds(pl.multiple_of(hh * hd, hd), hd)
        gt_hi[here, :] = t_hi
        gt_lo[here, :] = t_lo
        return carry

    lax.fori_loop(0, heads, finish_head, 0)
    out_copy = pltpu.make_async_copy(oq, gq_hbm, out_sem)
    out_copy.start()

    low_f, high_f = pl.ds(0, half_f), pl.ds(half_f, half_f)

    def sums(m, part=None):
        first, count = (0, feats) if part is None else (part * half_f, half_f)
        return kv.at[pl.ds(pl.multiple_of(m * feats + first, 8), count)]

    def core_out(n):
        return gbuf.at[pl.ds(pl.multiple_of((n % 4) * feats, 8), feats)]

    def core_copy(n):
        return rcopy(core_out(n), core_in.at[n % 4], cs.at[n], cr.at[n], mate)

    y_far_lo, y_far_hi, y_near_up, y_near_down = 0, 1, 2, 3

    def y_copy(m, slot, kind):
        if kind == y_far_lo:
            src, dst, dev = sums(m, 0), y_in.at[slot, 0, low_f], to_y_up
        elif kind == y_far_hi:
            src, dst, dev = sums(m, 1), y_in.at[slot, 0, high_f], to_y_down
        elif kind == y_near_up:
            src, dst, dev = sums(m), y_in.at[slot, 1], to_y_up
        else:
            src, dst, dev = sums(m), y_in.at[slot, 2], to_y_down
        return rcopy(src, dst, ys.at[slot, kind], yr.at[slot, kind], dev)

    def z_copy(m, slot, kind):
        if kind == 0:
            src, dst, dev = sums(m, 0), z_in.at[slot, 0, low_f], to_z_up
        elif kind == 1:
            src, dst, dev = sums(m, 1), z_in.at[slot, 1, high_f], to_z_down
        elif kind == 2:
            src, dst, dev = sums(m), z_in.at[slot, 1], to_z_down
        else:
            src, dst, dev = sums(m), z_in.at[slot, 0], to_z_up
        return rcopy(src, dst, zs.at[slot, kind], zr.at[slot, kind], dev)

    last_unit = (3, 10, 11, 15)
    block_of = (h, h_down, h_up, (h + 2) % 4)

    def z_dist(slot):
        return (z + 4 - block_of[slot]) % 4

    def z_first(slot):
        m = last_unit[slot]

        @pl.when(z_dist(slot) == 2)
        def _():
            z_copy(m, slot, 0).start()
            z_copy(m, slot, 1).start()

    def z_middle(slot):
        m = last_unit[slot]

        @pl.when(z_dist(slot) == 1)
        def _():
            z_copy(m, slot, 1).wait_recv()
            s = sums(m, 1)
            s[...] = s[...] + z_in[slot, 1, half_f:, :]
            z_copy(m, slot, 2).start()

        @pl.when(z_dist(slot) == 3)
        def _():
            z_copy(m, slot, 0).wait_recv()
            s = sums(m, 0)
            s[...] = s[...] + z_in[slot, 0, :half_f, :]
            z_copy(m, slot, 3).start()

    def z_root(slot):
        m = last_unit[slot]

        @pl.when(z_dist(slot) == 0)
        def _():
            z_copy(m, slot, 2).wait_recv()
            z_copy(m, slot, 3).wait_recv()
            s = sums(m)
            wq_ref[...] = (s[...] + z_in[slot, 0] + z_in[slot, 1]).T

    def z_drain(slot):
        m = last_unit[slot]

        @pl.when(z_dist(slot) == 2)
        def _():
            z_copy(m, slot, 0).wait_send()
            z_copy(m, slot, 1).wait_send()

        @pl.when(z_dist(slot) == 1)
        def _():
            z_copy(m, slot, 2).wait_send()

        @pl.when(z_dist(slot) == 3)
        def _():
            z_copy(m, slot, 3).wait_send()

    def place(m):
        near = jnp.logical_and(m >= 4, m < 12)
        slot = jnp.where(m < 4, 0, jnp.where(m < 12, 1 + m % 2, 3))
        j = jnp.where(near, (m - 4) // 2, m % 4)
        return slot, j

    def settle(m):
        slot, j = place(m)
        core_copy(m).wait_recv()
        s = sums(m)
        s[...] = s[...] + core_in[m % 4]

        @pl.when(j == 0)
        def _():
            y_copy(m, slot, y_far_lo).start()
            y_copy(m, slot, y_far_hi).start()

        @pl.when(j == 1)
        def _():
            y_copy(m, slot, y_far_lo).wait_recv()
            t = sums(m, 0)
            t[...] = t[...] + y_in[slot, 0, :half_f, :]
            y_copy(m, slot, y_near_up).start()

        @pl.when(j == 2)
        def _():
            y_copy(m, slot, y_far_hi).wait_recv()
            t = sums(m, 1)
            t[...] = t[...] + y_in[slot, 0, half_f:, :]
            y_copy(m, slot, y_near_down).start()

        @pl.when(j == 3)
        def _():
            y_copy(m, slot, y_near_up).wait_recv()
            y_copy(m, slot, y_near_down).wait_recv()
            t = sums(m)
            t[...] = t[...] + y_in[slot, 1] + y_in[slot, 2]

    def unit(n, carry):
        slot, j = place(n)

        @pl.when(slot == 0)
        def _():
            pltpu.make_async_copy(x_cols(0), xbuf.at[n], own_sem.at[j]).wait()

        @pl.when(slot == 1)
        def _():
            rcopy(x_cols(0), xbuf.at[n], xs.at[0, j], xr.at[0, j], to_h_up).wait_recv()
            x_right2(j).start()

        @pl.when(slot == 2)
        def _():
            rcopy(x_cols(0), xbuf.at[n], xs.at[1, j], xr.at[1, j], to_h_down).wait_recv()
            x_left2(j).start()

        @pl.when(slot == 3)
        def _():
            x_right2(j).wait_recv()
            x_left2(j).wait_recv()

        hi, lo = split(xbuf[n])
        x_hi[...] = hi
        x_lo[...] = lo

        @pl.when(n >= 4)
        def _():
            core_copy(n - 4).wait_send()

        def rows_of(ft, c2):
            rows = pl.ds(pl.multiple_of(ft * tile, tile), tile)
            a_hi = gt_hi[rows, :]
            acc = mm(a_hi, x_hi[...]) + mm(a_hi, x_lo[...]) + mm(gt_lo[rows, :], x_hi[...])
            left, right = acc[:, :128], acc[:, 128:]
            first = core == 0
            kv[pl.ds(pl.multiple_of(n * feats + ft * tile, tile), tile), :] = jnp.where(first, left, right)
            gbuf[pl.ds(pl.multiple_of((n % 4) * feats + ft * tile, tile), tile), :] = jnp.where(first, right, left)
            return c2

        lax.fori_loop(0, feats // tile, rows_of, 0)
        core_copy(n).start()

        @pl.when(n >= 1)
        def _():
            settle(n - 1)

        for slot_k, (a, b, c) in enumerate(((4, 6, 9), (11, 13, 15), (12, 14, 15))):
            @pl.when(n == a)
            def _():
                z_first(slot_k)

            @pl.when(n == b)
            def _():
                z_middle(slot_k)

            @pl.when(n == c)
            def _():
                z_root(slot_k)

        return carry

    lax.fori_loop(0, 16, unit, 0)
    settle(15)
    z_first(3)
    z_middle(3)
    z_root(3)

    out_copy.wait()
    for j in range(4):
        x_right(j).wait_send()
        x_left(j).wait_send()
        x_right2(j).wait_send()
        x_left2(j).wait_send()
    for p in range(1, 5):
        share(p).wait_send()
    for n in range(12, 16):
        core_copy(n).wait_send()
    for slot in range(4):
        first = (0, 4, 5, 12)[slot]
        by = (1, 2, 2, 1)[slot]
        y_copy(first, slot, y_far_lo).wait_send()
        y_copy(first, slot, y_far_hi).wait_send()
        y_copy(first + by, slot, y_near_up).wait_send()
        y_copy(first + 2 * by, slot, y_near_down).wait_send()
        z_drain(slot)


def body(tokens_x, keys, values, grad_out, level_table, level_bins):
    tokens, heads, hd = keys.shape
    feats = heads * hd
    used = (tokens * lax.axis_size("seq")).bit_length()
    table = jnp.transpose(level_table[:, :, :used], (0, 2, 1))
    quarter = tokens // 4
    dma = pltpu.SemaphoreType.DMA
    stack = max(tokens * heads * 2, 16 * feats)
    hbm = pl.BlockSpec(memory_space=pl.ANY)
    vmem = pl.BlockSpec(memory_space=pltpu.VMEM)
    gq, wq = pl.pallas_call(
        kernel,
        out_shape=(
            jax.ShapeDtypeStruct((tokens * heads, hd), F32),
            jax.ShapeDtypeStruct((128, feats), F32),
        ),
        in_specs=[hbm, hbm, hbm, hbm, vmem, vmem],
        out_specs=(hbm, vmem),
        scratch_shapes=[
            pltpu.VMEM((16, tokens, 256), F32),
            pltpu.VMEM((stack, hd), F32),
            pltpu.VMEM((max(tokens * heads, 4 * feats), hd), F32),
            pltpu.VMEM((tokens * heads, hd), F32),
            pltpu.VMEM((feats, tokens), BF16),
            pltpu.VMEM((feats, tokens), BF16),
            pltpu.VMEM((heads, used, tokens), F32),
            pltpu.VMEM((quarter, quarter), jnp.int32),
            pltpu.VMEM((heads, 4, hd, hd), F32),
            pltpu.VMEM((heads, hd, hd), F32),
            pltpu.VMEM((5, heads, hd, hd), F32),
            pltpu.VMEM((4, feats, 128), F32),
            pltpu.VMEM((4, 3, feats, 128), F32),
            pltpu.VMEM((4, 2, feats, 128), F32),
            pltpu.VMEM((tokens, 256), BF16),
            pltpu.VMEM((tokens, 256), BF16),
            dma((3,)),
            dma,
            dma((4,)),
            dma((4, 4)),
            dma((4, 4)),
            dma((5,)),
            dma((5,)),
            dma((5,)),
            dma((5,)),
            dma((16,)),
            dma((16,)),
            dma((4, 4)),
            dma((4, 4)),
            dma((4, 4)),
            dma((4, 4)),
        ],
        compiler_params=pltpu.CompilerParams(
            collective_id=0, has_side_effects=True, vmem_limit_bytes=63 * 1024 * 1024,
        ),
        name="query_grad",
    )(
        tokens_x,
        keys.reshape(tokens * heads, hd),
        values.reshape(tokens * heads, hd),
        grad_out.reshape(tokens * heads, hd),
        table,
        level_bins.T,
    )
    return gq.reshape(tokens, heads, hd), wq


def solution(mesh):
    in_specs = (
        P("seq", "head"),
        P("seq", "head", None),
        P("seq", "head", None),
        P("seq", "head", None),
        P("head", None, None),
        P("seq", "head"),
    )
    out_specs = (P("seq", "head", None), P("seq", "head"))
    return jax.shard_map(body, mesh=mesh, in_specs=in_specs, out_specs=out_specs, check_vma=False)
```

```python
import jax
import jax.numpy as jnp
from jax import lax
from jax.experimental import pallas as pl
from jax.experimental.pallas import tpu as pltpu
from jax.sharding import PartitionSpec as P

MESH = pl.DeviceIdType.MESH
F32 = jnp.float32
BF16 = jnp.bfloat16
NT = (((1,), (1,)), ((), ()))
NN = (((1,), (0,)), ((), ()))


def split(a):
    high = a.astype(BF16)
    return high, (a - high.astype(F32)).astype(BF16)


def mm(a, b, dims=NN):
    return lax.dot_general(a, b, dims, preferred_element_type=F32)


def kernel(
    x_hbm, k_hbm, v_hbm, g_hbm, tab_ref, bins_ref,
    gq_hbm, wq_ref,
    xbuf, kv, gbuf, oq, gt_hi, gt_lo, wts, lev, chunk_st, state, bucket,
    core_in, y_in, z_in, z_hop, x_hi, x_lo,
    load_sem, out_sem, own_sem, xs, xr, bs, br, ss, sr, cs, cr, ys, yr, zs, zr, zh,
):
    tokens, width = x_hbm.shape
    heads = tab_ref.shape[0]
    hd = 128
    feats = heads * hd
    quarter = tokens // 4
    half_t = tokens // 2
    half_f, quart_f = feats // 2, feats // 4
    half_h = heads // 2
    span_bits = tokens.bit_length() - 1
    tile = min(256, feats)

    seq = lax.axis_index("seq")
    h = lax.axis_index("head")
    z, y, core = seq // 8, (seq // 2) % 4, seq % 2

    def at(zz, yy, cc):
        return zz * 8 + yy * 2 + cc

    y_up, y_down = (y + 1) % 4, (y + 3) % 4
    z_up, z_down = (z + 1) % 4, (z + 3) % 4
    h_up, h_down = (h + 1) % 4, (h + 3) % 4
    mate = (at(z, y, 1 - core), h)
    to_y_up, to_y_down = (at(z, y_up, core), h), (at(z, y_down, core), h)
    to_z_up, to_z_down = (at(z_up, y, core), h), (at(z_down, y, core), h)
    to_h_up, to_h_down = (seq, h_up), (seq, h_down)
    y_flip = y + 1 - 2 * (y % 2)
    z_flip = z + 1 - 2 * (z % 2)
    y_far, z_far = (y + 2) % 4, (z + 2) % 4
    flips = [
        mate,
        (at(z, y_flip, core), h),
        (at(z, y_far, core), h),
        (at(z_flip, y, core), h),
        (at(z_far, y, core), h),
    ]
    friends = [
        mate, to_y_up, to_y_down, to_z_up, to_z_down, to_h_up, to_h_down, flips[2], flips[4],
    ]

    def rcopy(src, dst, ssem, rsem, dev):
        return pltpu.make_async_remote_copy(
            src_ref=src, dst_ref=dst, send_sem=ssem, recv_sem=rsem,
            device_id=dev, device_id_type=MESH,
        )

    loads = [
        pltpu.make_async_copy(v_hbm, kv.at[pl.ds(tokens * heads, tokens * heads)], load_sem.at[0]),
        pltpu.make_async_copy(k_hbm, kv.at[pl.ds(0, tokens * heads)], load_sem.at[1]),
        pltpu.make_async_copy(g_hbm, gbuf.at[pl.ds(0, tokens * heads)], load_sem.at[2]),
    ]
    for c in loads:
        c.start()

    barrier = pltpu.get_barrier_semaphore()
    for f in friends:
        pl.semaphore_signal(barrier, inc=1, device_id=f, device_id_type=MESH)
    pl.semaphore_wait(barrier, len(friends))

    offsets = (2, 1, 3, 0)

    def x_cols(j):
        yt = (y + offsets[j]) % 4
        return x_hbm.at[:, pl.ds(pl.multiple_of(yt * 256, 256), 256)]

    def x_own(j):
        return pltpu.make_async_copy(x_cols(j), xbuf.at[j], own_sem.at[j])

    def x_right(j):
        return rcopy(x_cols(j), xbuf.at[4 + 2 * j], xs.at[0, j], xr.at[0, j], to_h_up)

    def x_left(j):
        return rcopy(x_cols(j), xbuf.at[5 + 2 * j], xs.at[1, j], xr.at[1, j], to_h_down)

    low_t, high_t = pl.ds(0, half_t), pl.ds(half_t, half_t)

    def x_second(j, part, near, rows, kind, dev):
        cols = pl.ds(0, 256) if part is None else pl.ds(part * 128, 128)
        sem = j if part is None else 3 + part
        return rcopy(
            xbuf.at[near + 2 * j, rows, cols], xbuf.at[12 + j, rows, cols],
            xs.at[kind, sem], xr.at[kind, sem], dev)

    def x_right2(j, part=None):
        return x_second(j, part, 4, low_t, 2, to_h_up)

    def x_left2(j, part=None):
        return x_second(j, part, 5, high_t, 3, to_h_down)

    for j in range(4):
        x_right(j).start()
        x_left(j).start()
    for j in range(4):
        x_own(j).start()

    loads[0].wait()
    loads[1].wait()

    def head_rows(hh, first=0):
        return pl.ds(first + hh, tokens, stride=heads)

    def states_of(hh, carry):
        kh = kv[head_rows(hh), :]
        vh = kv[head_rows(hh, tokens * heads), :]
        total = None
        for c in range(4):
            rows = slice(c * quarter, (c + 1) * quarter)
            k_hi, k_lo = split(kh[rows])
            v_hi, v_lo = split(vh[rows].T)
            both = mm(v_hi, jnp.concatenate([k_hi, k_lo], axis=1))
            st = both[:, :hd] + both[:, hd:] + mm(v_lo, k_hi)
            chunk_st[hh, c] = st
            total = st if total is None else total + st
        state[hh] = total
        return carry

    lax.fori_loop(0, heads, states_of, 0)

    mine_h = pl.ds(core * half_h, half_h)
    other_h = pl.ds((1 - core) * half_h, half_h)

    def climb(p):
        if p == 0:
            return rcopy(state, bucket.at[0], bs.at[0], br.at[0], mate)
        return rcopy(state.at[mine_h], bucket.at[p, mine_h], bs.at[p], br.at[p], flips[p])

    def share(p):
        return rcopy(bucket.at[p, mine_h], bucket.at[p, mine_h], ss.at[p], sr.at[p], mate)

    def share_in(p):
        return rcopy(bucket.at[p, other_h], bucket.at[p, other_h], ss.at[p], sr.at[p], mate)

    def pump(p):
        climb(p).wait_recv()
        if p > 0:
            share(p).start()
            share_in(p).wait_recv()
        climb(p).wait_send()
        if p < 4:
            state[...] = state[...] + bucket[p]
            climb(p + 1).start()

    climb(0).start()

    for hh in range(heads):
        row = bins_ref[hh:hh + 1, :]
        tab = tab_ref[hh]
        acc = jnp.zeros((tab.shape[0], tokens), F32)
        for b in range(tab.shape[1]):
            acc = acc + jnp.where(row == b, tab[:, b:b + 1], 0.0)
        wts[hh] = acc

    later = lax.broadcasted_iota(jnp.int32, (quarter, quarter), 0)
    earlier = lax.broadcasted_iota(jnp.int32, (quarter, quarter), 1)
    differ = later ^ earlier
    digits = jnp.zeros((quarter, quarter), jnp.int32)
    for place in range(span_bits - 2):
        digits = digits + jnp.where(differ >= (1 << place), 1, 0)
    lev[...] = jnp.where(earlier <= later, digits, -1)

    loads[2].wait()

    def local_of(hh, carry):
        kh = kv[head_rows(hh), :]
        vh = kv[head_rows(hh, tokens * heads), :]
        gh = gbuf[head_rows(hh), :]
        levels = lev[...]
        parts = []
        for c in range(4):
            rows = slice(c * quarter, (c + 1) * quarter)
            k_hi, k_lo = split(kh[rows])
            v_hi, v_lo = split(vh[rows])
            g_hi, g_lo = split(gh[rows])
            g_two = jnp.concatenate([g_hi, g_lo], axis=1)
            scores = mm(g_two, jnp.concatenate([v_hi, v_hi], axis=1), NT) + mm(g_hi, v_lo, NT)
            w = wts[hh, :, rows].T
            mix = jnp.zeros((quarter, quarter), F32)
            for level in range(span_bits - 1):
                mix = jnp.where(levels == level, w[:, level:level + 1], mix)
            m_hi, m_lo = split(scores * mix)
            both = mm(m_hi, jnp.concatenate([k_hi, k_lo], axis=1))
            out = both[:, :hd] + both[:, hd:] + mm(m_lo, k_hi)

            def read(st):
                s_hi, s_lo = split(st)
                return mm(g_two, jnp.concatenate([s_hi, s_hi], axis=0)) + mm(g_hi, s_lo)

            if c % 2:
                out = out + w[:, span_bits - 1:span_bits] * read(chunk_st[hh, c - 1])
            if c >= 2:
                out = out + w[:, span_bits:span_bits + 1] * read(chunk_st[hh, 0] + chunk_st[hh, 1])
            parts.append(out)
        oq[head_rows(hh), :] = jnp.concatenate(parts, axis=0)

        @pl.when(hh == heads // 4 - 1)
        def _():
            pump(0)

        @pl.when(hh == heads - 2)
        def _():
            pump(1)

        return carry

    if heads >= 4:
        lax.fori_loop(0, heads, local_of, 0)
    else:
        for hh in range(heads):
            local_of(hh, 0)
        pump(0)
        pump(1)

    bits = [core, y % 2, y // 2, z % 2, z // 2]

    def read_pair(p):
        on_a = jnp.where(bits[p] == 1, 1.0, 0.0).astype(F32)
        on_b = jnp.where(bits[p + 1] == 1, 1.0, 0.0).astype(F32)
        first = span_bits + 1 + p

        def step(hh, carry):
            g_hi, g_lo = split(gbuf[head_rows(hh), :])
            g_two = jnp.concatenate([g_hi, g_lo], axis=1)
            s_hi, s_lo = split(jnp.concatenate([bucket[p, hh] * on_a, bucket[p + 1, hh] * on_b], axis=1))
            got = mm(g_two, jnp.concatenate([s_hi, s_hi], axis=0)) + mm(g_hi, s_lo)
            w = wts[hh].T
            oq[head_rows(hh), :] = (
                oq[head_rows(hh), :]
                + w[:, first:first + 1] * got[:, :hd]
                + w[:, first + 1:first + 2] * got[:, hd:]
            )
            return carry

        lax.fori_loop(0, heads, step, 0)

    pump(2)
    read_pair(0)
    pump(3)
    read_pair(2)
    pump(4)

    on_last = jnp.where(bits[4] == 1, 1.0, 0.0).astype(F32)

    def finish_head(hh, carry):
        g_hi, g_lo = split(gbuf[head_rows(hh), :])
        g_two = jnp.concatenate([g_hi, g_lo], axis=1)
        s_hi, s_lo = split(bucket[4, hh] * on_last)
        got = mm(g_two, jnp.concatenate([s_hi, s_hi], axis=0)) + mm(g_hi, s_lo)
        last = span_bits + 5
        done = oq[head_rows(hh), :] + wts[hh].T[:, last:last + 1] * got
        oq[head_rows(hh), :] = done
        t_hi, t_lo = split(done.T)
        here = pl.ds(pl.multiple_of(hh * hd, hd), hd)
        gt_hi[here, :] = t_hi
        gt_lo[here, :] = t_lo
        return carry

    lax.fori_loop(0, heads, finish_head, 0)
    out_copy = pltpu.make_async_copy(oq, gq_hbm, out_sem)
    out_copy.start()

    split_at = 15

    def sums(m, first=0, count=feats):
        return kv.at[pl.ds(pl.multiple_of(m * feats + first, 8), count)]

    def upper(m, first=0, count=half_f):
        return sums(m, half_f + first, count)

    def core_out(m):
        return gbuf.at[pl.ds(pl.multiple_of((m % 4) * feats, 8), feats)]

    def core_copy(m):
        return rcopy(core_out(m), core_in.at[m % 4], cs.at[m], cr.at[m], mate)

    lo, hi = pl.ds(0, quart_f), pl.ds(quart_f, quart_f)

    def y_copy(job, kind, src):
        dst = (
            y_in.at[job, 0, lo], y_in.at[job, 0, hi], y_in.at[job, 1, hi],
            y_in.at[job, 1, lo], y_in.at[job, 2, lo], y_in.at[job, 2, hi],
        )[kind]
        dev = (to_y_up, to_y_down, to_y_up, to_y_up, to_y_down, to_y_down)[kind]
        return rcopy(src, dst, ys.at[job, kind], yr.at[job, kind], dev)

    def y_step(job, rows, m, j):
        first, second, both = rows(m, 0, quart_f), rows(m, quart_f, quart_f), rows(m, 0, half_f)

        @pl.when(j == 0)
        def _():
            y_copy(job, 0, first).start()
            y_copy(job, 1, second).start()

        @pl.when(j == 1)
        def _():
            y_copy(job, 2, second).start()
            y_copy(job, 0, first).wait_recv()
            first[...] = first[...] + y_in[job, 0, :quart_f, :]
            y_copy(job, 3, first).start()

        @pl.when(j == 2)
        def _():
            y_copy(job, 4, first).start()
            y_copy(job, 1, second).wait_recv()
            second[...] = second[...] + y_in[job, 0, quart_f:, :]
            y_copy(job, 5, second).start()

        @pl.when(j == 3)
        def _():
            for kind in range(2, 6):
                y_copy(job, kind, first).wait_recv()
            both[...] = both[...] + y_in[job, 1] + y_in[job, 2]

    def z_far(job, kind, src):
        dev = (to_z_up, to_z_down)[kind]
        return rcopy(src, z_hop.at[job], zs.at[job, kind], zh.at[job], dev)

    def z_near(job, place, kind, src):
        side, part, dev = ((1, lo, to_z_down), (1, hi, to_z_down), (0, hi, to_z_up), (0, lo, to_z_up))[kind]
        return rcopy(src, z_in.at[place, side, part], zs.at[job, kind % 2], zr.at[place, kind], dev)

    def z_first(job, place, rows, m, dist):
        first, second = rows(m, 0, quart_f), rows(m, quart_f, quart_f)

        @pl.when(dist == 2)
        def _():
            z_far(job, 0, first).start()
            z_far(job, 1, second).start()

        @pl.when(dist == 1)
        def _():
            z_near(job, place, 0, first).start()

        @pl.when(dist == 3)
        def _():
            z_near(job, place, 2, second).start()

    def z_middle(job, place, rows, m, dist):
        first, second = rows(m, 0, quart_f), rows(m, quart_f, quart_f)

        @pl.when(dist == 1)
        def _():
            z_far(job, 1, second).wait_recv()
            second[...] = second[...] + z_hop[job]
            z_near(job, place, 1, second).start()

        @pl.when(dist == 3)
        def _():
            z_far(job, 0, first).wait_recv()
            first[...] = first[...] + z_hop[job]
            z_near(job, place, 3, first).start()

    def z_root(job, place, rows, m):
        both = rows(m, 0, half_f)
        for kind in range(4):
            z_near(job, place, kind, rows(m, 0, quart_f)).wait_recv()
        both[...] = both[...] + z_in[place, 0] + z_in[place, 1]

    def place_of(m):
        near = jnp.logical_and(m >= 4, m < 12)
        slot = jnp.where(m < 4, 0, jnp.where(m < 12, 1 + m % 2, 3))
        j = jnp.where(near, (m - 4) // 2, m % 4)
        block = jnp.where(slot == 0, h, jnp.where(slot == 1, h + 3, jnp.where(slot == 2, h + 1, h + 2)))
        return slot, j, (z + 8 - block) % 4

    def when_mine(step, act):
        halves = jnp.where(step == split_at, core == 0, core == 1)
        mine = jnp.logical_and(
            jnp.logical_and(step >= 0, step <= split_at + 1),
            jnp.logical_or(step < split_at, halves),
        )

        @pl.when(mine)
        def _():
            m = jnp.where(step > split_at, split_at, step)
            act(m, *place_of(m))

    def stage_one(m, slot, j, dist):
        core_copy(m).wait_recv()
        s = sums(m)
        s[...] = s[...] + core_in[m % 4]
        z_first(m, j, upper, m, dist)
        y_step(slot, sums, m, j)

        @pl.when(j == 3)
        def _():
            z_first(16 + slot, 4, sums, m, dist)

    def stage_two(m, slot, j, dist):
        z_middle(m, j, upper, m, dist)

        @pl.when(j == 3)
        def _():
            z_middle(16 + slot, 4, sums, m, dist)

    def stage_three(m, slot, j, dist):
        @pl.when(dist == 0)
        def _():
            z_root(m, j, upper, m)
            y_step(4, upper, m, j)

            @pl.when(j == 3)
            def _():
                z_root(16 + slot, 4, sums, m)
                wq_ref[...] = sums(m)[...].T

    def times(rows, cols):
        a_hi = gt_hi[rows, :]
        return (
            mm(a_hi, x_hi[:, cols]) + mm(a_hi, x_lo[:, cols]) + mm(gt_lo[rows, :], x_hi[:, cols])
        )

    def tile_rows(ft, m=0):
        return pl.ds(pl.multiple_of(m * feats + ft * tile, tile), tile)

    def arrive(n):
        slot, j, _ = place_of(n)

        @pl.when(slot == 0)
        def _():
            pltpu.make_async_copy(x_cols(0), xbuf.at[n], own_sem.at[j]).wait()

        @pl.when(slot == 1)
        def _():
            rcopy(x_cols(0), xbuf.at[n], xs.at[0, j], xr.at[0, j], to_h_up).wait_recv()

            @pl.when(j < 3)
            def _():
                x_right2(j).start()

            @pl.when(j == 3)
            def _():
                x_right2(3, 0).start()
                x_right2(3, 1).start()

        @pl.when(slot == 2)
        def _():
            rcopy(x_cols(0), xbuf.at[n], xs.at[1, j], xr.at[1, j], to_h_down).wait_recv()

            @pl.when(j < 3)
            def _():
                x_left2(j).start()

            @pl.when(j == 3)
            def _():
                x_left2(3, 0).start()
                x_left2(3, 1).start()

        @pl.when(slot == 3)
        def _():
            x_right2(j).wait_recv()
            x_left2(j).wait_recv()

    def whole_unit(n):
        arrive(n)
        high, low = split(xbuf[n])
        x_hi[...] = high
        x_lo[...] = low

        @pl.when(n >= 4)
        def _():
            core_copy(n - 4).wait_send()

        def rows_of(ft, c2):
            acc = times(tile_rows(ft), slice(0, 256))
            left, right = acc[:, :128], acc[:, 128:]
            first = core == 0
            kv[tile_rows(ft, n), :] = jnp.where(first, left, right)
            gbuf[tile_rows(ft, n % 4), :] = jnp.where(first, right, left)
            return c2

        lax.fori_loop(0, feats // tile, rows_of, 0)
        core_copy(n).start()

    def half_unit(n):
        part = n - split_at

        @pl.when(part == 0)
        def _():
            x_right2(3, 0).wait_recv()
            x_left2(3, 0).wait_recv()
            core_copy(split_at - 4).wait_send()

        @pl.when(part == 1)
        def _():
            x_right2(3, 1).wait_recv()
            x_left2(3, 1).wait_recv()

        high, low = split(xbuf[split_at, :, pl.ds(pl.multiple_of(part * 128, 128), 128)])
        x_hi[:, :128] = high
        x_lo[:, :128] = low

        def kept(ft, c2):
            kv[tile_rows(ft, split_at), :] = times(tile_rows(ft), slice(0, 128))
            return c2

        def given(ft, c2):
            gbuf[tile_rows(ft, split_at % 4), :] = times(tile_rows(ft), slice(0, 128))
            return c2

        @pl.when(core == part)
        def _():
            lax.fori_loop(0, feats // tile, kept, 0)

        @pl.when(core != part)
        def _():
            lax.fori_loop(0, feats // tile, given, 0)
            core_copy(split_at).start()

    def step(n, carry):
        @pl.when(n < split_at)
        def _():
            whole_unit(n)

        @pl.when(jnp.logical_or(n == split_at, n == split_at + 1))
        def _():
            half_unit(n)

        when_mine(n - 1, stage_one)
        when_mine(n - 2, stage_two)
        when_mine(n - 3, stage_three)
        return carry

    lax.fori_loop(0, split_at + 5, step, 0)

    out_copy.wait()
    for j in range(4):
        x_right(j).wait_send()
        x_left(j).wait_send()
    for j, part in ((0, None), (1, None), (2, None), (3, 0), (3, 1)):
        x_right2(j, part).wait_send()
        x_left2(j, part).wait_send()
    for p in range(1, 5):
        share(p).wait_send()
    for m in range(12, 16):
        core_copy(m).wait_send()

    def y_drain(job, carry):
        for kind in range(6):
            y_copy(job, kind, sums(0, 0, quart_f)).wait_send()
        return carry

    def z_drain(job, carry):
        m = jnp.where(job < 16, job, jnp.where(job == 16, 0, jnp.where(job == 19, 12, job - 13)))
        _, _, dist = place_of(m)

        @pl.when(dist != 0)
        def _():
            for kind in range(2):
                z_far(job, kind, sums(0, 0, quart_f)).wait_send()

        return carry

    lax.fori_loop(0, 5, y_drain, 0)
    lax.fori_loop(0, 20, z_drain, 0)


def body(tokens_x, keys, values, grad_out, level_table, level_bins):
    tokens, heads, hd = keys.shape
    feats = heads * hd
    used = (tokens * lax.axis_size("seq")).bit_length()
    table = jnp.transpose(level_table[:, :, :used], (0, 2, 1))
    quarter = tokens // 4
    dma = pltpu.SemaphoreType.DMA
    stack = max(tokens * heads * 2, 16 * feats)
    hbm = pl.BlockSpec(memory_space=pl.ANY)
    vmem = pl.BlockSpec(memory_space=pltpu.VMEM)
    gq, wq = pl.pallas_call(
        kernel,
        out_shape=(
            jax.ShapeDtypeStruct((tokens * heads, hd), F32),
            jax.ShapeDtypeStruct((128, feats), F32),
        ),
        in_specs=[hbm, hbm, hbm, hbm, vmem, vmem],
        out_specs=(hbm, vmem),
        scratch_shapes=[
            pltpu.VMEM((16, tokens, 256), F32),
            pltpu.VMEM((stack, hd), F32),
            pltpu.VMEM((max(tokens * heads, 4 * feats), hd), F32),
            pltpu.VMEM((tokens * heads, hd), F32),
            pltpu.VMEM((feats, tokens), BF16),
            pltpu.VMEM((feats, tokens), BF16),
            pltpu.VMEM((heads, used, tokens), F32),
            pltpu.VMEM((quarter, quarter), jnp.int32),
            pltpu.VMEM((heads, 4, hd, hd), F32),
            pltpu.VMEM((heads, hd, hd), F32),
            pltpu.VMEM((5, heads, hd, hd), F32),
            pltpu.VMEM((4, feats, 128), F32),
            pltpu.VMEM((5, 3, feats // 2, 128), F32),
            pltpu.VMEM((5, 2, feats // 2, 128), F32),
            pltpu.VMEM((20, feats // 4, 128), F32),
            pltpu.VMEM((tokens, 256), BF16),
            pltpu.VMEM((tokens, 256), BF16),
            dma((3,)),
            dma,
            dma((4,)),
            dma((4, 5)),
            dma((4, 5)),
            dma((5,)),
            dma((5,)),
            dma((5,)),
            dma((5,)),
            dma((16,)),
            dma((16,)),
            dma((5, 6)),
            dma((5, 6)),
            dma((20, 2)),
            dma((5, 4)),
            dma((20,)),
        ],
        compiler_params=pltpu.CompilerParams(
            collective_id=0, has_side_effects=True, vmem_limit_bytes=63 * 1024 * 1024,
        ),
        name="query_grad",
    )(
        tokens_x,
        keys.reshape(tokens * heads, hd),
        values.reshape(tokens * heads, hd),
        grad_out.reshape(tokens * heads, hd),
        table,
        level_bins.T,
    )
    return gq.reshape(tokens, heads, hd), wq


def solution(mesh):
    in_specs = (
        P("seq", "head"),
        P("seq", "head", None),
        P("seq", "head", None),
        P("seq", "head", None),
        P("head", None, None),
        P("seq", "head"),
    )
    out_specs = (P("seq", "head", None), P("seq", "head"))
    return jax.shard_map(body, mesh=mesh, in_specs=in_specs, out_specs=out_specs, check_vma=False)
```

```python
import jax
import jax.numpy as jnp
from jax import lax
from jax.experimental import pallas as pl
from jax.experimental.pallas import tpu as pltpu
from jax.sharding import PartitionSpec as P

MESH = pl.DeviceIdType.MESH
F32 = jnp.float32
BF16 = jnp.bfloat16
NT = (((1,), (1,)), ((), ()))
NN = (((1,), (0,)), ((), ()))


def split(a):
    high = a.astype(BF16)
    return high, (a - high.astype(F32)).astype(BF16)


def mm(a, b, dims=NN):
    return lax.dot_general(a, b, dims, preferred_element_type=F32)


def kernel(
    x_hbm, k_hbm, v_hbm, g_hbm, tab_ref, bins_ref,
    gq_hbm, wq_ref,
    xbuf, kv, gbuf, oq, gt_hi, gt_lo, wts, lev, chunk_st, state, bucket,
    core_in, y_in, z_in, z_hop, x_hi, x_lo,
    load_sem, out_sem, own_sem, xs, xr, bs, br, ss, sr, cs, cr, ys, yr, zs, zr, zh,
):
    tokens, width = x_hbm.shape
    heads = tab_ref.shape[0]
    hd = 128
    feats = heads * hd
    quarter = tokens // 4
    half_t = tokens // 2
    half_f, quart_f = feats // 2, feats // 4
    half_h = heads // 2
    span_bits = tokens.bit_length() - 1
    tile = min(256, feats)

    seq = lax.axis_index("seq")
    h = lax.axis_index("head")
    z, y, core = seq // 8, (seq // 2) % 4, seq % 2

    def at(zz, yy, cc):
        return zz * 8 + yy * 2 + cc

    y_up, y_down = (y + 1) % 4, (y + 3) % 4
    z_up, z_down = (z + 1) % 4, (z + 3) % 4
    h_up, h_down = (h + 1) % 4, (h + 3) % 4
    mate = (at(z, y, 1 - core), h)
    to_y_up, to_y_down = (at(z, y_up, core), h), (at(z, y_down, core), h)
    to_z_up, to_z_down = (at(z_up, y, core), h), (at(z_down, y, core), h)
    to_h_up, to_h_down = (seq, h_up), (seq, h_down)
    y_flip = y + 1 - 2 * (y % 2)
    z_flip = z + 1 - 2 * (z % 2)
    y_far, z_far = (y + 2) % 4, (z + 2) % 4
    flips = [
        mate,
        (at(z, y_flip, core), h),
        (at(z, y_far, core), h),
        (at(z_flip, y, core), h),
        (at(z_far, y, core), h),
    ]
    friends = [
        mate, to_y_up, to_y_down, to_z_up, to_z_down, to_h_up, to_h_down, flips[2], flips[4],
    ]

    def rcopy(src, dst, ssem, rsem, dev):
        return pltpu.make_async_remote_copy(
            src_ref=src, dst_ref=dst, send_sem=ssem, recv_sem=rsem,
            device_id=dev, device_id_type=MESH,
        )

    loads = [
        pltpu.make_async_copy(v_hbm, kv.at[pl.ds(tokens * heads, tokens * heads)], load_sem.at[0]),
        pltpu.make_async_copy(k_hbm, kv.at[pl.ds(0, tokens * heads)], load_sem.at[1]),
        pltpu.make_async_copy(g_hbm, gbuf.at[pl.ds(0, tokens * heads)], load_sem.at[2]),
    ]
    for c in loads:
        c.start()

    barrier = pltpu.get_barrier_semaphore()
    for f in friends:
        pl.semaphore_signal(barrier, inc=1, device_id=f, device_id_type=MESH)
    pl.semaphore_wait(barrier, len(friends))

    offsets = (2, 1, 3, 0)

    def x_cols(j):
        yt = (y + offsets[j]) % 4
        return x_hbm.at[:, pl.ds(pl.multiple_of(yt * 256, 256), 256)]

    def x_own(j):
        return pltpu.make_async_copy(x_cols(j), xbuf.at[3 * j], own_sem.at[j])

    def x_right(j):
        return rcopy(x_cols(j), xbuf.at[3 * j + 1], xs.at[0, j], xr.at[0, j], to_h_up)

    def x_left(j):
        return rcopy(x_cols(j), xbuf.at[3 * j + 2], xs.at[1, j], xr.at[1, j], to_h_down)

    low_t, high_t = pl.ds(0, half_t), pl.ds(half_t, half_t)

    def x_second(j, part, near, rows, kind, dev):
        cols = pl.ds(0, 256) if part is None else pl.ds(part * 128, 128)
        sem = j if part is None else 3 + part
        return rcopy(
            xbuf.at[near + 3 * j, rows, cols], xbuf.at[12 + j, rows, cols],
            xs.at[kind, sem], xr.at[kind, sem], dev)

    def x_right2(j, part=None):
        return x_second(j, part, 1, low_t, 2, to_h_up)

    def x_left2(j, part=None):
        return x_second(j, part, 2, high_t, 3, to_h_down)

    for j in range(4):
        x_right(j).start()
        x_left(j).start()
    for j in range(4):
        x_own(j).start()

    loads[0].wait()
    loads[1].wait()

    def head_rows(hh, first=0):
        return pl.ds(first + hh, tokens, stride=heads)

    def states_of(hh, carry):
        kh = kv[head_rows(hh), :]
        vh = kv[head_rows(hh, tokens * heads), :]
        total = None
        for c in range(4):
            rows = slice(c * quarter, (c + 1) * quarter)
            k_hi, k_lo = split(kh[rows])
            v_hi, v_lo = split(vh[rows].T)
            both = mm(v_hi, jnp.concatenate([k_hi, k_lo], axis=1))
            st = both[:, :hd] + both[:, hd:] + mm(v_lo, k_hi)
            chunk_st[hh, c] = st
            total = st if total is None else total + st
        state[hh] = total
        return carry

    lax.fori_loop(0, heads, states_of, 0)

    mine_h = pl.ds(core * half_h, half_h)
    other_h = pl.ds((1 - core) * half_h, half_h)

    def climb(p):
        if p == 0:
            return rcopy(state, bucket.at[0], bs.at[0], br.at[0], mate)
        return rcopy(state.at[mine_h], bucket.at[p, mine_h], bs.at[p], br.at[p], flips[p])

    def share(p):
        return rcopy(bucket.at[p, mine_h], bucket.at[p, mine_h], ss.at[p], sr.at[p], mate)

    def share_in(p):
        return rcopy(bucket.at[p, other_h], bucket.at[p, other_h], ss.at[p], sr.at[p], mate)

    def pump(p):
        climb(p).wait_recv()
        if p > 0:
            share(p).start()
            share_in(p).wait_recv()
        climb(p).wait_send()
        if p < 4:
            state[...] = state[...] + bucket[p]
            climb(p + 1).start()

    climb(0).start()

    for hh in range(heads):
        row = bins_ref[hh:hh + 1, :]
        tab = tab_ref[hh][:, :wts.shape[1]].T
        acc = jnp.zeros((tab.shape[0], tokens), F32)
        for b in range(tab.shape[1]):
            acc = acc + jnp.where(row == b, tab[:, b:b + 1], 0.0)
        wts[hh] = acc

    later = lax.broadcasted_iota(jnp.int32, (quarter, quarter), 0)
    earlier = lax.broadcasted_iota(jnp.int32, (quarter, quarter), 1)
    differ = later ^ earlier
    digits = jnp.zeros((quarter, quarter), jnp.int32)
    for place in range(span_bits - 2):
        digits = digits + jnp.where(differ >= (1 << place), 1, 0)
    lev[...] = jnp.where(earlier <= later, digits, -1)

    loads[2].wait()

    def local_of(hh, carry):
        kh = kv[head_rows(hh), :]
        vh = kv[head_rows(hh, tokens * heads), :]
        gh = gbuf[head_rows(hh), :]
        levels = lev[...]
        parts = []
        for c in range(4):
            rows = slice(c * quarter, (c + 1) * quarter)
            k_hi, k_lo = split(kh[rows])
            v_hi, v_lo = split(vh[rows])
            g_hi, g_lo = split(gh[rows])
            g_two = jnp.concatenate([g_hi, g_lo], axis=1)
            scores = mm(g_two, jnp.concatenate([v_hi, v_hi], axis=1), NT) + mm(g_hi, v_lo, NT)
            w = wts[hh, :, rows].T
            mix = jnp.zeros((quarter, quarter), F32)
            for level in range(span_bits - 1):
                mix = jnp.where(levels == level, w[:, level:level + 1], mix)
            m_hi, m_lo = split(scores * mix)
            both = mm(m_hi, jnp.concatenate([k_hi, k_lo], axis=1))
            out = both[:, :hd] + both[:, hd:] + mm(m_lo, k_hi)

            def read(st):
                s_hi, s_lo = split(st)
                return mm(g_two, jnp.concatenate([s_hi, s_hi], axis=0)) + mm(g_hi, s_lo)

            if c % 2:
                out = out + w[:, span_bits - 1:span_bits] * read(chunk_st[hh, c - 1])
            if c >= 2:
                out = out + w[:, span_bits:span_bits + 1] * read(chunk_st[hh, 0] + chunk_st[hh, 1])
            parts.append(out)
        oq[head_rows(hh), :] = jnp.concatenate(parts, axis=0)

        @pl.when(hh == heads // 2 - 1)
        def _():
            pump(1)

        return carry

    pump(0)
    lax.fori_loop(0, heads, local_of, 0)

    bits = [core, y % 2, y // 2, z % 2, z // 2]

    def read_pair(p):
        on_a = jnp.where(bits[p] == 1, 1.0, 0.0).astype(F32)
        on_b = jnp.where(bits[p + 1] == 1, 1.0, 0.0).astype(F32)
        first = span_bits + 1 + p

        def step(hh, carry):
            g_hi, g_lo = split(gbuf[head_rows(hh), :])
            g_two = jnp.concatenate([g_hi, g_lo], axis=1)
            s_hi, s_lo = split(jnp.concatenate([bucket[p, hh] * on_a, bucket[p + 1, hh] * on_b], axis=1))
            got = mm(g_two, jnp.concatenate([s_hi, s_hi], axis=0)) + mm(g_hi, s_lo)
            w = wts[hh].T
            oq[head_rows(hh), :] = (
                oq[head_rows(hh), :]
                + w[:, first:first + 1] * got[:, :hd]
                + w[:, first + 1:first + 2] * got[:, hd:]
            )
            return carry

        lax.fori_loop(0, heads, step, 0)

    pump(2)
    read_pair(0)
    pump(3)
    read_pair(2)
    pump(4)

    on_last = jnp.where(bits[4] == 1, 1.0, 0.0).astype(F32)

    def finish_head(hh, carry):
        g_hi, g_lo = split(gbuf[head_rows(hh), :])
        g_two = jnp.concatenate([g_hi, g_lo], axis=1)
        s_hi, s_lo = split(bucket[4, hh] * on_last)
        got = mm(g_two, jnp.concatenate([s_hi, s_hi], axis=0)) + mm(g_hi, s_lo)
        last = span_bits + 5
        done = oq[head_rows(hh), :] + wts[hh].T[:, last:last + 1] * got
        oq[head_rows(hh), :] = done
        t_hi, t_lo = split(done.T)
        here = pl.ds(pl.multiple_of(hh * hd, hd), hd)
        gt_hi[here, :] = t_hi
        gt_lo[here, :] = t_lo
        return carry

    lax.fori_loop(0, heads, finish_head, 0)
    out_copy = pltpu.make_async_copy(oq, gq_hbm, out_sem)
    out_copy.start()

    split_at = 15

    def sums(m, first=0, count=feats):
        return kv.at[pl.ds(pl.multiple_of(m * feats + first, 8), count)]

    def upper(m, first=0, count=half_f):
        return sums(m, half_f + first, count)

    def core_out(m):
        return gbuf.at[pl.ds(pl.multiple_of((m % 4) * feats, 8), feats)]

    def core_copy(m):
        return rcopy(core_out(m), core_in.at[m % 4], cs.at[m], cr.at[m], mate)

    def last_core_copy(part):
        slot, rows = split_at % 4, pl.ds(part * half_f, half_f)
        return rcopy(
            gbuf.at[pl.ds(slot * feats + part * half_f, half_f)], core_in.at[slot, rows],
            cs.at[split_at + part], cr.at[split_at + part], mate)

    lo, hi = pl.ds(0, quart_f), pl.ds(quart_f, quart_f)

    def y_copy(job, kind, src):
        dst = (
            y_in.at[job, 0, lo], y_in.at[job, 0, hi], y_in.at[job, 1, hi],
            y_in.at[job, 1, lo], y_in.at[job, 2, lo], y_in.at[job, 2, hi],
        )[kind]
        dev = (to_y_up, to_y_down, to_y_up, to_y_up, to_y_down, to_y_down)[kind]
        return rcopy(src, dst, ys.at[job, kind], yr.at[job, kind], dev)

    def y_step(job, rows, m, j):
        first, second, both = rows(m, 0, quart_f), rows(m, quart_f, quart_f), rows(m, 0, half_f)

        @pl.when(j == 0)
        def _():
            y_copy(job, 0, first).start()
            y_copy(job, 1, second).start()

        @pl.when(j == 1)
        def _():
            y_copy(job, 2, second).start()
            y_copy(job, 0, first).wait_recv()
            first[...] = first[...] + y_in[job, 0, :quart_f, :]
            y_copy(job, 3, first).start()

        @pl.when(j == 2)
        def _():
            y_copy(job, 4, first).start()
            y_copy(job, 1, second).wait_recv()
            second[...] = second[...] + y_in[job, 0, quart_f:, :]
            y_copy(job, 5, second).start()

        @pl.when(j == 3)
        def _():
            for kind in range(2, 6):
                y_copy(job, kind, first).wait_recv()
            both[...] = both[...] + y_in[job, 1] + y_in[job, 2]

    def z_far(job, kind, src):
        dev = (to_z_up, to_z_down)[kind]
        return rcopy(src, z_hop.at[job], zs.at[job, kind], zh.at[job], dev)

    def z_near(job, place, kind, src):
        side, part, dev = ((1, lo, to_z_down), (1, hi, to_z_down), (0, hi, to_z_up), (0, lo, to_z_up))[kind]
        return rcopy(src, z_in.at[place, side, part], zs.at[job, kind % 2], zr.at[place, kind], dev)

    def z_first(job, place, rows, m, dist):
        first, second = rows(m, 0, quart_f), rows(m, quart_f, quart_f)

        @pl.when(dist == 2)
        def _():
            z_far(job, 0, first).start()
            z_far(job, 1, second).start()

        @pl.when(dist == 1)
        def _():
            z_near(job, place, 0, first).start()

        @pl.when(dist == 3)
        def _():
            z_near(job, place, 2, second).start()

    def z_middle(job, place, rows, m, dist):
        first, second = rows(m, 0, quart_f), rows(m, quart_f, quart_f)

        @pl.when(dist == 1)
        def _():
            z_far(job, 1, second).wait_recv()
            second[...] = second[...] + z_hop[job]
            z_near(job, place, 1, second).start()

        @pl.when(dist == 3)
        def _():
            z_far(job, 0, first).wait_recv()
            first[...] = first[...] + z_hop[job]
            z_near(job, place, 3, first).start()

    def z_root(job, place, rows, m):
        both = rows(m, 0, half_f)
        for kind in range(4):
            z_near(job, place, kind, rows(m, 0, quart_f)).wait_recv()
        both[...] = both[...] + z_in[place, 0] + z_in[place, 1]

    def dist_of(slot):
        block = jnp.where(slot == 0, h, jnp.where(slot == 1, h + 3, jnp.where(slot == 2, h + 1, h + 2)))
        return (z + 8 - block) % 4

    def place_of(m):
        slot = jnp.where(m < 12, m % 3, 3)
        return slot, jnp.where(m < 12, m // 3, m - 12), dist_of(slot)

    def when_mine(step, act):
        halves = jnp.where(step == split_at, core == 0, core == 1)
        mine = jnp.logical_and(
            jnp.logical_and(step >= 0, step <= split_at + 1),
            jnp.logical_or(step < split_at, halves),
        )

        @pl.when(mine)
        def _():
            m = jnp.where(step > split_at, split_at, step)
            act(m, *place_of(m))

    def stage_one(m, slot, j, dist):
        @pl.when(m < split_at)
        def _():
            core_copy(m).wait_recv()

        @pl.when(m == split_at)
        def _():
            last_core_copy(0).wait_recv()

        s = sums(m, 0, half_f)
        s[...] = s[...] + core_in[m % 4, :half_f, :]
        y_step(slot, sums, m, j)

        @pl.when(j == 3)
        def _():
            z_first(16 + slot, 4, sums, m, dist)

        @pl.when(m == split_at)
        def _():
            last_core_copy(1).wait_recv()

        s = upper(m)
        s[...] = s[...] + core_in[m % 4, half_f:, :]
        z_first(m, j, upper, m, dist)

    def stage_two(m, slot, j, dist):
        @pl.when(j == 3)
        def _():
            z_middle(16 + slot, 4, sums, m, dist)

        z_middle(m, j, upper, m, dist)

    def stage_three(m, slot, j, dist):
        @pl.when(dist == 0)
        def _():
            z_root(m, j, upper, m)
            y_step(4, upper, m, j)

            @pl.when(j == 3)
            def _():
                z_root(16 + slot, 4, sums, m)
                wq_ref[...] = sums(m)[...].T

    def times(rows):
        a_hi = gt_hi[rows, :]
        return mm(a_hi, x_hi[...]) + mm(a_hi, x_lo[...]) + mm(gt_lo[rows, :], x_hi[...])

    def tile_rows(ft, m=0):
        return pl.ds(pl.multiple_of(m * feats + ft * tile, tile), tile)

    def arrive(n):
        slot, j, _ = place_of(n)

        @pl.when(slot == 0)
        def _():
            pltpu.make_async_copy(x_cols(0), xbuf.at[n], own_sem.at[j]).wait()

        @pl.when(slot == 1)
        def _():
            rcopy(x_cols(0), xbuf.at[n], xs.at[0, j], xr.at[0, j], to_h_up).wait_recv()

            @pl.when(j < 3)
            def _():
                x_right2(j).start()

            @pl.when(j == 3)
            def _():
                x_right2(3, 0).start()
                x_right2(3, 1).start()

        @pl.when(slot == 2)
        def _():
            rcopy(x_cols(0), xbuf.at[n], xs.at[1, j], xr.at[1, j], to_h_down).wait_recv()

            @pl.when(j < 3)
            def _():
                x_left2(j).start()

            @pl.when(j == 3)
            def _():
                x_left2(3, 0).start()
                x_left2(3, 1).start()

        @pl.when(slot == 3)
        def _():
            x_right2(j).wait_recv()
            x_left2(j).wait_recv()

    def whole_unit(n):
        arrive(n)
        high, low = split(xbuf[n])
        x_hi[...] = high
        x_lo[...] = low

        @pl.when(n >= 4)
        def _():
            core_copy(n - 4).wait_send()

        def rows_of(ft, c2):
            acc = times(tile_rows(ft))
            left, right = acc[:, :128], acc[:, 128:]
            first = core == 0
            kv[tile_rows(ft, n), :] = jnp.where(first, left, right)
            gbuf[tile_rows(ft, n % 4), :] = jnp.where(first, right, left)
            return c2

        lax.fori_loop(0, feats // tile, rows_of, 0)
        core_copy(n).start()

    def half_unit(n):
        part = n - split_at

        @pl.when(part == 0)
        def _():
            x_right2(3, 0).wait_recv()
            x_left2(3, 0).wait_recv()
            core_copy(split_at - 4).wait_send()

        @pl.when(part == 1)
        def _():
            x_right2(3, 1).wait_recv()
            x_left2(3, 1).wait_recv()

        high, low = split(xbuf[split_at, :, pl.ds(pl.multiple_of(part * 128, 128), 128)])
        x_hi[:, :128] = high
        x_hi[:, 128:] = low

        def narrow(rows):
            both = mm(gt_hi[rows, :], x_hi[...])
            return both[:, :128] + both[:, 128:] + mm(gt_lo[rows, :], x_hi[:, :128])

        def kept(ft, c2):
            kv[tile_rows(ft, split_at), :] = narrow(tile_rows(ft))
            return c2

        def given(ft, c2):
            gbuf[tile_rows(ft, split_at % 4), :] = narrow(tile_rows(ft))

            @pl.when(ft == tiles // 2 - 1)
            def _():
                last_core_copy(0).start()

            return c2

        tiles = feats // tile

        @pl.when(core == part)
        def _():
            lax.fori_loop(0, tiles, kept, 0)

        @pl.when(core != part)
        def _():
            lax.fori_loop(0, tiles, given, 0)
            last_core_copy(1).start()

    def due(t, lag, late):
        m = jnp.where(jnp.logical_and(t >= lag, t < 12 + lag), t - lag, -1)
        for i, when in enumerate(late):
            m = jnp.where(t == when, 12 + i, m)
        return m

    def step(t, carry):
        n = due(t, 0, (17, 20, 23, 26, 28))

        @pl.when(jnp.logical_and(n >= 0, n < split_at))
        def _():
            whole_unit(n)

        @pl.when(n >= split_at)
        def _():
            half_unit(n)

        when_mine(due(t, 1, (18, 21, 24, 27, 29)), stage_one)
        when_mine(due(t, 3, (19, 22, 25, 28, 30)), stage_two)
        when_mine(due(t, 5, (20, 23, 26, 30, 31)), stage_three)
        return carry

    lax.fori_loop(0, 32, step, 0)

    out_copy.wait()
    for j in range(4):
        x_right(j).wait_send()
        x_left(j).wait_send()
    for j, part in ((0, None), (1, None), (2, None), (3, 0), (3, 1)):
        x_right2(j, part).wait_send()
        x_left2(j, part).wait_send()
    for p in range(1, 5):
        share(p).wait_send()
    for m in range(12, 15):
        core_copy(m).wait_send()
    last_core_copy(0).wait_send()
    last_core_copy(1).wait_send()

    def y_drain(job, carry):
        for kind in range(6):
            y_copy(job, kind, sums(0, 0, quart_f)).wait_send()
        return carry

    def z_drain(job, carry):
        slot, _, _ = place_of(job)
        slot = jnp.where(job < 16, slot, job - 16)

        @pl.when(dist_of(slot) != 0)
        def _():
            for kind in range(2):
                z_far(job, kind, sums(0, 0, quart_f)).wait_send()

        return carry

    lax.fori_loop(0, 5, y_drain, 0)
    lax.fori_loop(0, 20, z_drain, 0)


def body(tokens_x, keys, values, grad_out, level_table, level_bins):
    tokens, heads, hd = keys.shape
    feats = heads * hd
    used = (tokens * lax.axis_size("seq")).bit_length()
    quarter = tokens // 4
    dma = pltpu.SemaphoreType.DMA
    stack = max(tokens * heads * 2, 16 * feats)
    hbm = pl.BlockSpec(memory_space=pl.ANY)
    vmem = pl.BlockSpec(memory_space=pltpu.VMEM)
    gq, wq = pl.pallas_call(
        kernel,
        out_shape=(
            jax.ShapeDtypeStruct((tokens * heads, hd), F32),
            jax.ShapeDtypeStruct((128, feats), F32),
        ),
        in_specs=[hbm, hbm, hbm, hbm, vmem, vmem],
        out_specs=(hbm, vmem),
        scratch_shapes=[
            pltpu.VMEM((16, tokens, 256), F32),
            pltpu.VMEM((stack, hd), F32),
            pltpu.VMEM((max(tokens * heads, 4 * feats), hd), F32),
            pltpu.VMEM((tokens * heads, hd), F32),
            pltpu.VMEM((feats, tokens), BF16),
            pltpu.VMEM((feats, tokens), BF16),
            pltpu.VMEM((heads, used, tokens), F32),
            pltpu.VMEM((quarter, quarter), jnp.int32),
            pltpu.VMEM((heads, 4, hd, hd), F32),
            pltpu.VMEM((heads, hd, hd), F32),
            pltpu.VMEM((5, heads, hd, hd), F32),
            pltpu.VMEM((4, feats, 128), F32),
            pltpu.VMEM((5, 3, feats // 2, 128), F32),
            pltpu.VMEM((5, 2, feats // 2, 128), F32),
            pltpu.VMEM((20, feats // 4, 128), F32),
            pltpu.VMEM((tokens, 256), BF16),
            pltpu.VMEM((tokens, 256), BF16),
            dma((3,)),
            dma,
            dma((4,)),
            dma((4, 5)),
            dma((4, 5)),
            dma((5,)),
            dma((5,)),
            dma((5,)),
            dma((5,)),
            dma((17,)),
            dma((17,)),
            dma((5, 6)),
            dma((5, 6)),
            dma((20, 2)),
            dma((5, 4)),
            dma((20,)),
        ],
        compiler_params=pltpu.CompilerParams(
            collective_id=0, has_side_effects=True, vmem_limit_bytes=63 * 1024 * 1024,
        ),
        name="query_grad",
    )(
        tokens_x,
        keys.reshape(tokens * heads, hd),
        values.reshape(tokens * heads, hd),
        grad_out.reshape(tokens * heads, hd),
        level_table,
        level_bins.T,
    )
    return gq.reshape(tokens, heads, hd), wq


def solution(mesh):
    in_specs = (
        P("seq", "head"),
        P("seq", "head", None),
        P("seq", "head", None),
        P("seq", "head", None),
        P("head", None, None),
        P("seq", "head"),
    )
    out_specs = (P("seq", "head", None), P("seq", "head"))
    return jax.shard_map(body, mesh=mesh, in_specs=in_specs, out_specs=out_specs, check_vma=False)
```

```python
import jax
import jax.numpy as jnp
from jax import lax
from jax.experimental import pallas as pl
from jax.experimental.pallas import tpu as pltpu
from jax.sharding import PartitionSpec as P

MESH = pl.DeviceIdType.MESH
F32 = jnp.float32
BF16 = jnp.bfloat16
NT = (((1,), (1,)), ((), ()))
NN = (((1,), (0,)), ((), ()))


def split(a):
    high = a.astype(BF16)
    return high, (a - high.astype(F32)).astype(BF16)


def mm(a, b, dims=NN):
    return lax.dot_general(a, b, dims, preferred_element_type=F32)


def kernel(
    x_hbm, k_hbm, v_hbm, g_hbm, tab_ref, bins_ref,
    gq_hbm, wq_ref,
    xbuf, kv, gbuf, oq, gt_hi, gt_lo, wts, lev, chunk_st, state, bucket,
    core_in, y_in, z_in, z_hop, x_hi, x_lo,
    load_sem, out_sem, own_sem, xs, xr, bs, br, ss, sr, cs, cr, ys, yr, zs, zr, zh,
):
    tokens, width = x_hbm.shape
    heads = tab_ref.shape[0]
    hd = 128
    feats = heads * hd
    quarter = tokens // 4
    half_t = tokens // 2
    half_f, quart_f = feats // 2, feats // 4
    half_h = heads // 2
    span_bits = tokens.bit_length() - 1
    tile = min(256, feats)

    seq = lax.axis_index("seq")
    h = lax.axis_index("head")
    z, y, core = seq // 8, (seq // 2) % 4, seq % 2

    def at(zz, yy, cc):
        return zz * 8 + yy * 2 + cc

    y_up, y_down = (y + 1) % 4, (y + 3) % 4
    z_up, z_down = (z + 1) % 4, (z + 3) % 4
    h_up, h_down = (h + 1) % 4, (h + 3) % 4
    mate = (at(z, y, 1 - core), h)
    to_y_up, to_y_down = (at(z, y_up, core), h), (at(z, y_down, core), h)
    to_z_up, to_z_down = (at(z_up, y, core), h), (at(z_down, y, core), h)
    to_h_up, to_h_down = (seq, h_up), (seq, h_down)
    y_flip = y + 1 - 2 * (y % 2)
    z_flip = z + 1 - 2 * (z % 2)
    y_far, z_far = (y + 2) % 4, (z + 2) % 4
    flips = [
        mate,
        (at(z, y_flip, core), h),
        (at(z, y_far, core), h),
        (at(z_flip, y, core), h),
        (at(z_far, y, core), h),
    ]
    friends = [
        mate, to_y_up, to_y_down, to_z_up, to_z_down, to_h_up, to_h_down, flips[2], flips[4],
    ]

    def rcopy(src, dst, ssem, rsem, dev):
        return pltpu.make_async_remote_copy(
            src_ref=src, dst_ref=dst, send_sem=ssem, recv_sem=rsem,
            device_id=dev, device_id_type=MESH,
        )

    loads = [
        pltpu.make_async_copy(v_hbm, kv.at[pl.ds(tokens * heads, tokens * heads)], load_sem.at[0]),
        pltpu.make_async_copy(k_hbm, kv.at[pl.ds(0, tokens * heads)], load_sem.at[1]),
        pltpu.make_async_copy(g_hbm, gbuf.at[pl.ds(0, tokens * heads)], load_sem.at[2]),
    ]
    for c in loads:
        c.start()

    barrier = pltpu.get_barrier_semaphore()
    for f in friends:
        pl.semaphore_signal(barrier, inc=1, device_id=f, device_id_type=MESH)
    pl.semaphore_wait(barrier, len(friends))

    offsets = (2, 1, 3, 0)

    def x_cols(j):
        yt = (y + offsets[j]) % 4
        return x_hbm.at[:, pl.ds(pl.multiple_of(yt * 256, 256), 256)]

    def x_own(j):
        return pltpu.make_async_copy(x_cols(j), xbuf.at[3 * j], own_sem.at[j])

    def x_right(j):
        return rcopy(x_cols(j), xbuf.at[3 * j + 1], xs.at[0, j], xr.at[0, j], to_h_up)

    def x_left(j):
        return rcopy(x_cols(j), xbuf.at[3 * j + 2], xs.at[1, j], xr.at[1, j], to_h_down)

    low_t, high_t = pl.ds(0, half_t), pl.ds(half_t, half_t)

    def x_second(j, part, near, rows, kind, dev):
        cols = pl.ds(0, 256) if part is None else pl.ds(part * 128, 128)
        sem = j if part is None else 3 + part
        return rcopy(
            xbuf.at[near + 3 * j, rows, cols], xbuf.at[12 + j, rows, cols],
            xs.at[kind, sem], xr.at[kind, sem], dev)

    def x_right2(j, part=None):
        return x_second(j, part, 1, low_t, 2, to_h_up)

    def x_left2(j, part=None):
        return x_second(j, part, 2, high_t, 3, to_h_down)

    for j in range(4):
        x_right(j).start()
        x_left(j).start()
    for j in range(4):
        x_own(j).start()

    loads[0].wait()
    loads[1].wait()

    def head_rows(hh, first=0):
        return pl.ds(first + hh, tokens, stride=heads)

    def states_of(hh, carry):
        kh = kv[head_rows(hh), :]
        vh = kv[head_rows(hh, tokens * heads), :]
        total = None
        for c in range(4):
            rows = slice(c * quarter, (c + 1) * quarter)
            k_hi, k_lo = split(kh[rows])
            v_hi, v_lo = split(vh[rows].T)
            both = mm(v_hi, jnp.concatenate([k_hi, k_lo], axis=1))
            st = both[:, :hd] + both[:, hd:] + mm(v_lo, k_hi)
            chunk_st[hh, c] = st
            total = st if total is None else total + st
        state[hh] = total
        return carry

    lax.fori_loop(0, heads, states_of, 0)

    mine_h = pl.ds(core * half_h, half_h)
    other_h = pl.ds((1 - core) * half_h, half_h)

    def climb(p):
        if p == 0:
            return rcopy(state, bucket.at[0], bs.at[0], br.at[0], mate)
        return rcopy(state.at[mine_h], bucket.at[p, mine_h], bs.at[p], br.at[p], flips[p])

    def share(p):
        return rcopy(bucket.at[p, mine_h], bucket.at[p, mine_h], ss.at[p], sr.at[p], mate)

    def share_in(p):
        return rcopy(bucket.at[p, other_h], bucket.at[p, other_h], ss.at[p], sr.at[p], mate)

    def pump(p):
        climb(p).wait_recv()
        if p > 0:
            share(p).start()
            share_in(p).wait_recv()
        climb(p).wait_send()
        if p < 4:
            state[...] = state[...] + bucket[p]
            climb(p + 1).start()

    climb(0).start()

    for hh in range(heads):
        row = bins_ref[hh:hh + 1, :]
        tab = tab_ref[hh][:, :wts.shape[1]].T
        acc = jnp.zeros((tab.shape[0], tokens), F32)
        for b in range(tab.shape[1]):
            acc = acc + jnp.where(row == b, tab[:, b:b + 1], 0.0)
        wts[hh] = acc

    later = lax.broadcasted_iota(jnp.int32, (quarter, quarter), 0)
    earlier = lax.broadcasted_iota(jnp.int32, (quarter, quarter), 1)
    differ = later ^ earlier
    digits = jnp.zeros((quarter, quarter), jnp.int32)
    for place in range(span_bits - 2):
        digits = digits + jnp.where(differ >= (1 << place), 1, 0)
    lev[...] = jnp.where(earlier <= later, digits, -1)

    loads[2].wait()

    def local_of(hh, carry):
        kh = kv[head_rows(hh), :]
        vh = kv[head_rows(hh, tokens * heads), :]
        gh = gbuf[head_rows(hh), :]
        levels = lev[...]
        parts = []
        for c in range(4):
            rows = slice(c * quarter, (c + 1) * quarter)
            k_hi, k_lo = split(kh[rows])
            v_hi, v_lo = split(vh[rows])
            g_hi, g_lo = split(gh[rows])
            g_two = jnp.concatenate([g_hi, g_lo], axis=1)
            scores = mm(g_two, jnp.concatenate([v_hi, v_hi], axis=1), NT) + mm(g_hi, v_lo, NT)
            w = wts[hh, :, rows].T
            mix = jnp.zeros((quarter, quarter), F32)
            for level in range(span_bits - 1):
                mix = jnp.where(levels == level, w[:, level:level + 1], mix)
            m_hi, m_lo = split(scores * mix)
            both = mm(m_hi, jnp.concatenate([k_hi, k_lo], axis=1))
            out = both[:, :hd] + both[:, hd:] + mm(m_lo, k_hi)

            def read(st):
                s_hi, s_lo = split(st)
                return mm(g_two, jnp.concatenate([s_hi, s_hi], axis=0)) + mm(g_hi, s_lo)

            if c % 2:
                out = out + w[:, span_bits - 1:span_bits] * read(chunk_st[hh, c - 1])
            if c >= 2:
                out = out + w[:, span_bits:span_bits + 1] * read(chunk_st[hh, 0] + chunk_st[hh, 1])
            parts.append(out)
        oq[head_rows(hh), :] = jnp.concatenate(parts, axis=0)

        @pl.when(hh == heads // 2 - 1)
        def _():
            pump(1)

        return carry

    pump(0)
    lax.fori_loop(0, heads, local_of, 0)

    bits = [core, y % 2, y // 2, z % 2, z // 2]

    def read_pair(p):
        on_a = jnp.where(bits[p] == 1, 1.0, 0.0).astype(F32)
        on_b = jnp.where(bits[p + 1] == 1, 1.0, 0.0).astype(F32)
        first = span_bits + 1 + p

        def step(hh, carry):
            g_hi, g_lo = split(gbuf[head_rows(hh), :])
            g_two = jnp.concatenate([g_hi, g_lo], axis=1)
            s_hi, s_lo = split(jnp.concatenate([bucket[p, hh] * on_a, bucket[p + 1, hh] * on_b], axis=1))
            got = mm(g_two, jnp.concatenate([s_hi, s_hi], axis=0)) + mm(g_hi, s_lo)
            w = wts[hh].T
            oq[head_rows(hh), :] = (
                oq[head_rows(hh), :]
                + w[:, first:first + 1] * got[:, :hd]
                + w[:, first + 1:first + 2] * got[:, hd:]
            )
            return carry

        lax.fori_loop(0, heads, step, 0)

    pump(2)
    read_pair(0)
    pump(3)
    read_pair(2)
    pump(4)

    on_last = jnp.where(bits[4] == 1, 1.0, 0.0).astype(F32)

    def finish_head(hh, carry):
        g_hi, g_lo = split(gbuf[head_rows(hh), :])
        g_two = jnp.concatenate([g_hi, g_lo], axis=1)
        s_hi, s_lo = split(bucket[4, hh] * on_last)
        got = mm(g_two, jnp.concatenate([s_hi, s_hi], axis=0)) + mm(g_hi, s_lo)
        last = span_bits + 5
        done = oq[head_rows(hh), :] + wts[hh].T[:, last:last + 1] * got
        oq[head_rows(hh), :] = done
        t_hi, t_lo = split(done.T)
        here = pl.ds(pl.multiple_of(hh * hd, hd), hd)
        gt_hi[here, :] = t_hi
        gt_lo[here, :] = t_lo
        return carry

    lax.fori_loop(0, heads, finish_head, 0)
    out_copy = pltpu.make_async_copy(oq, gq_hbm, out_sem)
    out_copy.start()

    split_at = 15

    def sums(m, first=0, count=feats):
        return kv.at[pl.ds(pl.multiple_of(m * feats + first, 8), count)]

    def upper(m, first=0, count=half_f):
        return sums(m, half_f + first, count)

    def core_out(m):
        return gbuf.at[pl.ds(pl.multiple_of((m % 4) * feats, 8), feats)]

    def core_copy(m):
        return rcopy(core_out(m), core_in.at[m % 4], cs.at[m], cr.at[m], mate)

    def last_core_copy(part):
        slot, rows = split_at % 4, pl.ds(part * half_f, half_f)
        return rcopy(
            gbuf.at[pl.ds(slot * feats + part * half_f, half_f)], core_in.at[slot, rows],
            cs.at[split_at + part], cr.at[split_at + part], mate)

    lo, hi = pl.ds(0, quart_f), pl.ds(quart_f, quart_f)

    def y_copy(job, kind, src):
        dst = (
            y_in.at[job, 0, lo], y_in.at[job, 0, hi], y_in.at[job, 1, hi],
            y_in.at[job, 1, lo], y_in.at[job, 2, lo], y_in.at[job, 2, hi],
        )[kind]
        dev = (to_y_up, to_y_down, to_y_up, to_y_up, to_y_down, to_y_down)[kind]
        return rcopy(src, dst, ys.at[job, kind], yr.at[job, kind], dev)

    def y_step(job, rows, m, j):
        first, second, both = rows(m, 0, quart_f), rows(m, quart_f, quart_f), rows(m, 0, half_f)

        @pl.when(j == 0)
        def _():
            y_copy(job, 0, first).start()
            y_copy(job, 1, second).start()

        @pl.when(j == 1)
        def _():
            y_copy(job, 2, second).start()
            y_copy(job, 0, first).wait_recv()
            first[...] = first[...] + y_in[job, 0, :quart_f, :]
            y_copy(job, 3, first).start()

        @pl.when(j == 2)
        def _():
            y_copy(job, 4, first).start()
            y_copy(job, 1, second).wait_recv()
            second[...] = second[...] + y_in[job, 0, quart_f:, :]
            y_copy(job, 5, second).start()

        @pl.when(j == 3)
        def _():
            for kind in range(2, 6):
                y_copy(job, kind, first).wait_recv()
            both[...] = both[...] + y_in[job, 1] + y_in[job, 2]

    def z_far(job, kind, src):
        dev = (to_z_up, to_z_down)[kind]
        return rcopy(src, z_hop.at[job], zs.at[job, kind], zh.at[job], dev)

    def z_near(job, place, kind, src):
        side, part, dev = ((1, lo, to_z_down), (1, hi, to_z_down), (0, hi, to_z_up), (0, lo, to_z_up))[kind]
        return rcopy(src, z_in.at[place, side, part], zs.at[job, kind % 2], zr.at[place, kind], dev)

    def z_first(job, place, rows, m, dist):
        first, second = rows(m, 0, quart_f), rows(m, quart_f, quart_f)

        @pl.when(dist == 2)
        def _():
            z_far(job, 0, first).start()
            z_far(job, 1, second).start()

        @pl.when(dist == 1)
        def _():
            z_near(job, place, 0, first).start()

        @pl.when(dist == 3)
        def _():
            z_near(job, place, 2, second).start()

    def z_middle(job, place, rows, m, dist):
        first, second = rows(m, 0, quart_f), rows(m, quart_f, quart_f)

        @pl.when(dist == 1)
        def _():
            z_far(job, 1, second).wait_recv()
            second[...] = second[...] + z_hop[job]
            z_near(job, place, 1, second).start()

        @pl.when(dist == 3)
        def _():
            z_far(job, 0, first).wait_recv()
            first[...] = first[...] + z_hop[job]
            z_near(job, place, 3, first).start()

    def z_root(job, place, rows, m):
        both = rows(m, 0, half_f)
        for kind in range(4):
            z_near(job, place, kind, rows(m, 0, quart_f)).wait_recv()
        both[...] = both[...] + z_in[place, 0] + z_in[place, 1]

    def dist_of(slot):
        block = jnp.where(slot == 0, h, jnp.where(slot == 1, h + 3, jnp.where(slot == 2, h + 1, h + 2)))
        return (z + 8 - block) % 4

    def place_of(m):
        slot = jnp.where(m < 12, m % 3, 3)
        return slot, jnp.where(m < 12, m // 3, m - 12), dist_of(slot)

    def when_mine(step, act):
        halves = jnp.where(step == split_at, core == 0, core == 1)
        mine = jnp.logical_and(
            jnp.logical_and(step >= 0, step <= split_at + 1),
            jnp.logical_or(step < split_at, halves),
        )

        @pl.when(mine)
        def _():
            m = jnp.where(step > split_at, split_at, step)
            act(m, *place_of(m))

    def stage_one(m, slot, j, dist):
        @pl.when(m < split_at)
        def _():
            core_copy(m).wait_recv()

        @pl.when(m == split_at)
        def _():
            last_core_copy(0).wait_recv()

        s = sums(m, 0, half_f)
        s[...] = s[...] + core_in[m % 4, :half_f, :]
        y_step(slot, sums, m, j)

        @pl.when(j == 3)
        def _():
            z_first(16 + slot, 4, sums, m, dist)

        @pl.when(m == split_at)
        def _():
            last_core_copy(1).wait_recv()

        s = upper(m)
        s[...] = s[...] + core_in[m % 4, half_f:, :]
        z_first(m, j, upper, m, dist)

    def stage_two(m, slot, j, dist):
        @pl.when(j == 3)
        def _():
            z_middle(16 + slot, 4, sums, m, dist)

        z_middle(m, j, upper, m, dist)

    def stage_three(m, slot, j, dist):
        @pl.when(dist == 0)
        def _():
            z_root(m, j, upper, m)
            y_step(4, upper, m, j)

            @pl.when(j == 3)
            def _():
                z_root(16 + slot, 4, sums, m)
                wq_ref[...] = sums(m)[...].T

    def times(rows):
        a_hi = gt_hi[rows, :]
        return mm(a_hi, x_hi[...]) + mm(a_hi, x_lo[...]) + mm(gt_lo[rows, :], x_hi[...])

    def tile_rows(ft, m=0):
        return pl.ds(pl.multiple_of(m * feats + ft * tile, tile), tile)

    def arrive(n):
        slot, j, _ = place_of(n)

        @pl.when(slot == 0)
        def _():
            pltpu.make_async_copy(x_cols(0), xbuf.at[n], own_sem.at[j]).wait()

        @pl.when(slot == 1)
        def _():
            rcopy(x_cols(0), xbuf.at[n], xs.at[0, j], xr.at[0, j], to_h_up).wait_recv()

            @pl.when(j < 3)
            def _():
                x_right2(j).start()

            @pl.when(j == 3)
            def _():
                x_right2(3, 0).start()
                x_right2(3, 1).start()

        @pl.when(slot == 2)
        def _():
            rcopy(x_cols(0), xbuf.at[n], xs.at[1, j], xr.at[1, j], to_h_down).wait_recv()

            @pl.when(j < 3)
            def _():
                x_left2(j).start()

            @pl.when(j == 3)
            def _():
                x_left2(3, 0).start()
                x_left2(3, 1).start()

        @pl.when(slot == 3)
        def _():
            x_right2(j).wait_recv()
            x_left2(j).wait_recv()

    def whole_unit(n):
        arrive(n)
        high, low = split(xbuf[n])
        x_hi[...] = high
        x_lo[...] = low

        @pl.when(n >= 4)
        def _():
            core_copy(n - 4).wait_send()

        def rows_of(ft, c2):
            acc = times(tile_rows(ft))
            left, right = acc[:, :128], acc[:, 128:]
            first = core == 0
            kv[tile_rows(ft, n), :] = jnp.where(first, left, right)
            gbuf[tile_rows(ft, n % 4), :] = jnp.where(first, right, left)
            return c2

        lax.fori_loop(0, feats // tile, rows_of, 0)
        core_copy(n).start()

    def half_unit(n):
        part = n - split_at

        @pl.when(part == 0)
        def _():
            x_right2(3, 0).wait_recv()
            x_left2(3, 0).wait_recv()
            core_copy(split_at - 4).wait_send()

        @pl.when(part == 1)
        def _():
            x_right2(3, 1).wait_recv()
            x_left2(3, 1).wait_recv()

        high, low = split(xbuf[split_at, :, pl.ds(pl.multiple_of(part * 128, 128), 128)])
        x_hi[:, :128] = high
        x_hi[:, 128:] = low

        def narrow(rows):
            both = mm(gt_hi[rows, :], x_hi[...])
            return both[:, :128] + both[:, 128:] + mm(gt_lo[rows, :], x_hi[:, :128])

        def kept(ft, c2):
            kv[tile_rows(ft, split_at), :] = narrow(tile_rows(ft))
            return c2

        def given(ft, c2):
            gbuf[tile_rows(ft, split_at % 4), :] = narrow(tile_rows(ft))

            @pl.when(ft == tiles // 2 - 1)
            def _():
                last_core_copy(0).start()

            return c2

        tiles = feats // tile

        @pl.when(core == part)
        def _():
            lax.fori_loop(0, tiles, kept, 0)

        @pl.when(core != part)
        def _():
            lax.fori_loop(0, tiles, given, 0)
            last_core_copy(1).start()

    def due(t, lag, late):
        m = jnp.where(jnp.logical_and(t >= lag, t < 12 + lag), t - lag, -1)
        for i, when in enumerate(late):
            m = jnp.where(t == when, 12 + i, m)
        return m

    def step(t, carry):
        n = due(t, 0, (17, 20, 23, 26, 28))

        @pl.when(jnp.logical_and(n >= 0, n < split_at))
        def _():
            whole_unit(n)

        @pl.when(n >= split_at)
        def _():
            half_unit(n)

        when_mine(due(t, 1, (18, 21, 24, 27, 29)), stage_one)
        when_mine(due(t, 3, (19, 22, 25, 28, 30)), stage_two)
        when_mine(due(t, 5, (20, 23, 26, 30, 31)), stage_three)
        return carry

    lax.fori_loop(0, 32, step, 0)

    out_copy.wait()
    for j in range(4):
        x_right(j).wait_send()
        x_left(j).wait_send()
    for j, part in ((0, None), (1, None), (2, None), (3, 0), (3, 1)):
        x_right2(j, part).wait_send()
        x_left2(j, part).wait_send()
    for p in range(1, 5):
        share(p).wait_send()
    for m in range(12, 15):
        core_copy(m).wait_send()
    last_core_copy(0).wait_send()
    last_core_copy(1).wait_send()

    def y_drain(job, carry):
        for kind in range(6):
            y_copy(job, kind, sums(0, 0, quart_f)).wait_send()
        return carry

    def z_drain(job, carry):
        slot, _, _ = place_of(job)
        slot = jnp.where(job < 16, slot, job - 16)

        @pl.when(dist_of(slot) != 0)
        def _():
            for kind in range(2):
                z_far(job, kind, sums(0, 0, quart_f)).wait_send()

        return carry

    lax.fori_loop(0, 5, y_drain, 0)
    lax.fori_loop(0, 20, z_drain, 0)


PIECES = 8


def hand_over(gq_in, wq_in, gq_out, wq_out, gq_buf, wq_buf, in_sem, out_sem):
    count = gq_buf.shape[0] // PIECES
    parts = [pl.ds(i * count, count) for i in range(PIECES)]
    fetch = [pltpu.make_async_copy(gq_in.at[p], gq_buf.at[p], in_sem.at[i]) for i, p in enumerate(parts)]
    store = [pltpu.make_async_copy(gq_buf.at[p], gq_out.at[p], out_sem.at[i]) for i, p in enumerate(parts)]
    fetch.append(pltpu.make_async_copy(wq_in, wq_buf, in_sem.at[PIECES]))
    store.append(pltpu.make_async_copy(wq_buf, wq_out, out_sem.at[PIECES]))
    for c in fetch:
        c.start()
    for f, c in zip(fetch, store):
        f.wait()
        c.start()
    for c in store:
        c.wait()


def body(tokens_x, keys, values, grad_out, level_table, level_bins):
    tokens, heads, hd = keys.shape
    feats = heads * hd
    used = (tokens * lax.axis_size("seq")).bit_length()
    quarter = tokens // 4
    dma = pltpu.SemaphoreType.DMA
    stack = max(tokens * heads * 2, 16 * feats)
    hbm = pl.BlockSpec(memory_space=pl.ANY)
    vmem = pl.BlockSpec(memory_space=pltpu.VMEM)
    gq, wq = pl.pallas_call(
        kernel,
        out_shape=(
            jax.ShapeDtypeStruct((tokens * heads, hd), F32),
            jax.ShapeDtypeStruct((128, feats), F32),
        ),
        in_specs=[hbm, hbm, hbm, hbm, vmem, vmem],
        out_specs=(hbm, vmem),
        scratch_shapes=[
            pltpu.VMEM((16, tokens, 256), F32),
            pltpu.VMEM((stack, hd), F32),
            pltpu.VMEM((max(tokens * heads, 4 * feats), hd), F32),
            pltpu.VMEM((tokens * heads, hd), F32),
            pltpu.VMEM((feats, tokens), BF16),
            pltpu.VMEM((feats, tokens), BF16),
            pltpu.VMEM((heads, used, tokens), F32),
            pltpu.VMEM((quarter, quarter), jnp.int32),
            pltpu.VMEM((heads, 4, hd, hd), F32),
            pltpu.VMEM((heads, hd, hd), F32),
            pltpu.VMEM((5, heads, hd, hd), F32),
            pltpu.VMEM((4, feats, 128), F32),
            pltpu.VMEM((5, 3, feats // 2, 128), F32),
            pltpu.VMEM((5, 2, feats // 2, 128), F32),
            pltpu.VMEM((20, feats // 4, 128), F32),
            pltpu.VMEM((tokens, 256), BF16),
            pltpu.VMEM((tokens, 256), BF16),
            dma((3,)),
            dma,
            dma((4,)),
            dma((4, 5)),
            dma((4, 5)),
            dma((5,)),
            dma((5,)),
            dma((5,)),
            dma((5,)),
            dma((17,)),
            dma((17,)),
            dma((5, 6)),
            dma((5, 6)),
            dma((20, 2)),
            dma((5, 4)),
            dma((20,)),
        ],
        compiler_params=pltpu.CompilerParams(
            collective_id=0, has_side_effects=True, vmem_limit_bytes=63 * 1024 * 1024,
        ),
        name="query_grad",
    )(
        tokens_x,
        keys.reshape(tokens * heads, hd),
        values.reshape(tokens * heads, hd),
        grad_out.reshape(tokens * heads, hd),
        level_table,
        level_bins.T,
    )
    rows = tokens * heads
    gq, wq = pl.pallas_call(
        hand_over,
        out_shape=(jax.ShapeDtypeStruct((rows, hd), F32), jax.ShapeDtypeStruct(wq.shape, F32)),
        in_specs=[hbm, hbm],
        out_specs=(hbm, hbm),
        scratch_shapes=[
            pltpu.VMEM((rows, hd), F32),
            pltpu.VMEM(wq.shape, F32),
            dma((PIECES + 1,)),
            dma((PIECES + 1,)),
        ],
        compiler_params=pltpu.CompilerParams(vmem_limit_bytes=62 * 1024 * 1024),
        name="hand_over",
    )(gq, wq)
    return gq.reshape(tokens, heads, hd), wq


def solution(mesh):
    in_specs = (
        P("seq", "head"),
        P("seq", "head", None),
        P("seq", "head", None),
        P("seq", "head", None),
        P("head", None, None),
        P("seq", "head"),
    )
    out_specs = (P("seq", "head", None), P("seq", "head"))
    return jax.shard_map(body, mesh=mesh, in_specs=in_specs, out_specs=out_specs, check_vma=False)
```

```python
import jax
import jax.numpy as jnp
from jax import lax
from jax.experimental import pallas as pl
from jax.experimental.pallas import tpu as pltpu
from jax.sharding import PartitionSpec as P

MESH = pl.DeviceIdType.MESH
F32 = jnp.float32
BF16 = jnp.bfloat16
NT = (((1,), (1,)), ((), ()))
NN = (((1,), (0,)), ((), ()))


def split(a):
    high = a.astype(BF16)
    return high, (a - high.astype(F32)).astype(BF16)


def mm(a, b, dims=NN):
    return lax.dot_general(a, b, dims, preferred_element_type=F32)


def kernel(
    x_hbm, k_hbm, v_hbm, g_hbm, tab_ref, bins_ref,
    gq_hbm, wq_ref,
    xbuf, kv, gbuf, oq, gt_hi, gt_lo, wts, lev, chunk_st, state, bucket,
    core_in, y_in, z_in, z_hop, x_hi, x_lo,
    load_sem, out_sem, own_sem, xs, xr, bs, br, ss, sr, cs, cr, ys, yr, zs, zr, zh,
):
    tokens, width = x_hbm.shape
    heads = tab_ref.shape[0]
    hd = 128
    feats = heads * hd
    quarter = tokens // 4
    half_t = tokens // 2
    half_f, quart_f = feats // 2, feats // 4
    half_h = heads // 2
    span_bits = tokens.bit_length() - 1
    tile = min(256, feats)

    seq = lax.axis_index("seq")
    h = lax.axis_index("head")
    z, y, core = seq // 8, (seq // 2) % 4, seq % 2

    def at(zz, yy, cc):
        return zz * 8 + yy * 2 + cc

    y_up, y_down = (y + 1) % 4, (y + 3) % 4
    z_up, z_down = (z + 1) % 4, (z + 3) % 4
    h_up, h_down = (h + 1) % 4, (h + 3) % 4
    mate = (at(z, y, 1 - core), h)
    to_y_up, to_y_down = (at(z, y_up, core), h), (at(z, y_down, core), h)
    to_z_up, to_z_down = (at(z_up, y, core), h), (at(z_down, y, core), h)
    to_h_up, to_h_down = (seq, h_up), (seq, h_down)
    y_flip = y + 1 - 2 * (y % 2)
    z_flip = z + 1 - 2 * (z % 2)
    y_far, z_far = (y + 2) % 4, (z + 2) % 4
    flips = [
        mate,
        (at(z, y_flip, core), h),
        (at(z, y_far, core), h),
        (at(z_flip, y, core), h),
        (at(z_far, y, core), h),
    ]
    friends = [
        mate, to_y_up, to_y_down, to_z_up, to_z_down, to_h_up, to_h_down, flips[2], flips[4],
    ]

    def rcopy(src, dst, ssem, rsem, dev):
        return pltpu.make_async_remote_copy(
            src_ref=src, dst_ref=dst, send_sem=ssem, recv_sem=rsem,
            device_id=dev, device_id_type=MESH,
        )

    loads = [
        pltpu.make_async_copy(v_hbm, kv.at[pl.ds(tokens * heads, tokens * heads)], load_sem.at[0]),
        pltpu.make_async_copy(k_hbm, kv.at[pl.ds(0, tokens * heads)], load_sem.at[1]),
        pltpu.make_async_copy(g_hbm, gbuf.at[pl.ds(0, tokens * heads)], load_sem.at[2]),
    ]
    for c in loads:
        c.start()

    barrier = pltpu.get_barrier_semaphore()
    for f in friends:
        pl.semaphore_signal(barrier, inc=1, device_id=f, device_id_type=MESH)
    pl.semaphore_wait(barrier, len(friends))

    offsets = (2, 1, 3, 0)

    def x_cols(j):
        yt = (y + offsets[j]) % 4
        return x_hbm.at[:, pl.ds(pl.multiple_of(yt * 256, 256), 256)]

    def x_own(j):
        return pltpu.make_async_copy(x_cols(j), xbuf.at[3 * j], own_sem.at[j])

    def x_right(j):
        return rcopy(x_cols(j), xbuf.at[3 * j + 1], xs.at[0, j], xr.at[0, j], to_h_up)

    def x_left(j):
        return rcopy(x_cols(j), xbuf.at[3 * j + 2], xs.at[1, j], xr.at[1, j], to_h_down)

    low_t, high_t = pl.ds(0, half_t), pl.ds(half_t, half_t)

    def x_second(j, part, near, rows, kind, dev):
        cols = pl.ds(0, 256) if part is None else pl.ds(part * 128, 128)
        sem = j if part is None else 3 + part
        return rcopy(
            xbuf.at[near + 3 * j, rows, cols], xbuf.at[12 + j, rows, cols],
            xs.at[kind, sem], xr.at[kind, sem], dev)

    def x_right2(j, part=None):
        return x_second(j, part, 1, low_t, 2, to_h_up)

    def x_left2(j, part=None):
        return x_second(j, part, 2, high_t, 3, to_h_down)

    for j in range(4):
        x_right(j).start()
        x_left(j).start()
    for j in range(4):
        x_own(j).start()

    loads[0].wait()
    loads[1].wait()

    def head_rows(hh, first=0):
        return pl.ds(first + hh, tokens, stride=heads)

    def states_of(hh, carry):
        kh = kv[head_rows(hh), :]
        vh = kv[head_rows(hh, tokens * heads), :]
        total = None
        for c in range(4):
            rows = slice(c * quarter, (c + 1) * quarter)
            k_hi, k_lo = split(kh[rows])
            v_hi, v_lo = split(vh[rows].T)
            both = mm(v_hi, jnp.concatenate([k_hi, k_lo], axis=1))
            st = both[:, :hd] + both[:, hd:] + mm(v_lo, k_hi)
            chunk_st[hh, c] = st
            total = st if total is None else total + st
        state[hh] = total
        return carry

    lax.fori_loop(0, heads, states_of, 0)

    mine_h = pl.ds(core * half_h, half_h)
    other_h = pl.ds((1 - core) * half_h, half_h)

    def climb(p):
        if p == 0:
            return rcopy(state, bucket.at[0], bs.at[0], br.at[0], mate)
        return rcopy(state.at[mine_h], bucket.at[p, mine_h], bs.at[p], br.at[p], flips[p])

    def share(p):
        return rcopy(bucket.at[p, mine_h], bucket.at[p, mine_h], ss.at[p], sr.at[p], mate)

    def share_in(p):
        return rcopy(bucket.at[p, other_h], bucket.at[p, other_h], ss.at[p], sr.at[p], mate)

    def pump(p):
        climb(p).wait_recv()
        if p > 0:
            share(p).start()
            share_in(p).wait_recv()
        climb(p).wait_send()
        if p < 4:
            state[...] = state[...] + bucket[p]
            climb(p + 1).start()

    climb(0).start()

    for hh in range(heads):
        row = bins_ref[hh:hh + 1, :]
        tab = tab_ref[hh][:, :wts.shape[1]].T
        acc = jnp.zeros((tab.shape[0], tokens), F32)
        for b in range(tab.shape[1]):
            acc = acc + jnp.where(row == b, tab[:, b:b + 1], 0.0)
        wts[hh] = acc

    later = lax.broadcasted_iota(jnp.int32, (quarter, quarter), 0)
    earlier = lax.broadcasted_iota(jnp.int32, (quarter, quarter), 1)
    differ = later ^ earlier
    digits = jnp.zeros((quarter, quarter), jnp.int32)
    for place in range(span_bits - 2):
        digits = digits + jnp.where(differ >= (1 << place), 1, 0)
    lev[...] = jnp.where(earlier <= later, digits, -1)

    loads[2].wait()

    def local_of(hh, carry):
        kh = kv[head_rows(hh), :]
        vh = kv[head_rows(hh, tokens * heads), :]
        gh = gbuf[head_rows(hh), :]
        levels = lev[...]
        parts = []
        for c in range(4):
            rows = slice(c * quarter, (c + 1) * quarter)
            k_hi, k_lo = split(kh[rows])
            v_hi, v_lo = split(vh[rows])
            g_hi, g_lo = split(gh[rows])
            g_two = jnp.concatenate([g_hi, g_lo], axis=1)
            scores = mm(g_two, jnp.concatenate([v_hi, v_hi], axis=1), NT) + mm(g_hi, v_lo, NT)
            w = wts[hh, :, rows].T
            mix = jnp.zeros((quarter, quarter), F32)
            for level in range(span_bits - 1):
                mix = jnp.where(levels == level, w[:, level:level + 1], mix)
            m_hi, m_lo = split(scores * mix)
            both = mm(m_hi, jnp.concatenate([k_hi, k_lo], axis=1))
            out = both[:, :hd] + both[:, hd:] + mm(m_lo, k_hi)

            def read(st):
                s_hi, s_lo = split(st)
                return mm(g_two, jnp.concatenate([s_hi, s_hi], axis=0)) + mm(g_hi, s_lo)

            if c % 2:
                out = out + w[:, span_bits - 1:span_bits] * read(chunk_st[hh, c - 1])
            if c >= 2:
                out = out + w[:, span_bits:span_bits + 1] * read(chunk_st[hh, 0] + chunk_st[hh, 1])
            parts.append(out)
        oq[head_rows(hh), :] = jnp.concatenate(parts, axis=0)

        @pl.when(hh == heads // 2 - 1)
        def _():
            pump(1)

        return carry

    pump(0)
    lax.fori_loop(0, heads, local_of, 0)

    bits = [core, y % 2, y // 2, z % 2, z // 2]

    def read_pair(p):
        on_a = jnp.where(bits[p] == 1, 1.0, 0.0).astype(F32)
        on_b = jnp.where(bits[p + 1] == 1, 1.0, 0.0).astype(F32)
        first = span_bits + 1 + p

        def step(hh, carry):
            g_hi, g_lo = split(gbuf[head_rows(hh), :])
            g_two = jnp.concatenate([g_hi, g_lo], axis=1)
            s_hi, s_lo = split(jnp.concatenate([bucket[p, hh] * on_a, bucket[p + 1, hh] * on_b], axis=1))
            got = mm(g_two, jnp.concatenate([s_hi, s_hi], axis=0)) + mm(g_hi, s_lo)
            w = wts[hh].T
            oq[head_rows(hh), :] = (
                oq[head_rows(hh), :]
                + w[:, first:first + 1] * got[:, :hd]
                + w[:, first + 1:first + 2] * got[:, hd:]
            )
            return carry

        lax.fori_loop(0, heads, step, 0)

    pump(2)
    read_pair(0)
    pump(3)
    read_pair(2)
    pump(4)

    on_last = jnp.where(bits[4] == 1, 1.0, 0.0).astype(F32)

    def finish_head(hh, carry):
        g_hi, g_lo = split(gbuf[head_rows(hh), :])
        g_two = jnp.concatenate([g_hi, g_lo], axis=1)
        s_hi, s_lo = split(bucket[4, hh] * on_last)
        got = mm(g_two, jnp.concatenate([s_hi, s_hi], axis=0)) + mm(g_hi, s_lo)
        last = span_bits + 5
        done = oq[head_rows(hh), :] + wts[hh].T[:, last:last + 1] * got
        oq[head_rows(hh), :] = done
        t_hi, t_lo = split(done.T)
        here = pl.ds(pl.multiple_of(hh * hd, hd), hd)
        gt_hi[here, :] = t_hi
        gt_lo[here, :] = t_lo
        return carry

    lax.fori_loop(0, heads, finish_head, 0)
    out_copy = pltpu.make_async_copy(oq, gq_hbm, out_sem)
    out_copy.start()

    split_at = 15

    def sums(m, first=0, count=feats):
        return kv.at[pl.ds(pl.multiple_of(m * feats + first, 8), count)]

    def upper(m, first=0, count=half_f):
        return sums(m, half_f + first, count)

    def core_out(m):
        return gbuf.at[pl.ds(pl.multiple_of((m % 4) * feats, 8), feats)]

    def core_copy(m):
        return rcopy(core_out(m), core_in.at[m % 4], cs.at[m], cr.at[m], mate)

    def last_core_copy(part):
        slot, rows = split_at % 4, pl.ds(part * half_f, half_f)
        return rcopy(
            gbuf.at[pl.ds(slot * feats + part * half_f, half_f)], core_in.at[slot, rows],
            cs.at[split_at + part], cr.at[split_at + part], mate)

    lo, hi = pl.ds(0, quart_f), pl.ds(quart_f, quart_f)

    def y_copy(job, kind, src):
        dst = (
            y_in.at[job, 0, lo], y_in.at[job, 0, hi], y_in.at[job, 1, hi],
            y_in.at[job, 1, lo], y_in.at[job, 2, lo], y_in.at[job, 2, hi],
        )[kind]
        dev = (to_y_up, to_y_down, to_y_up, to_y_up, to_y_down, to_y_down)[kind]
        return rcopy(src, dst, ys.at[job, kind], yr.at[job, kind], dev)

    def y_step(job, rows, m, j):
        first, second, both = rows(m, 0, quart_f), rows(m, quart_f, quart_f), rows(m, 0, half_f)

        @pl.when(j == 0)
        def _():
            y_copy(job, 0, first).start()
            y_copy(job, 1, second).start()

        @pl.when(j == 1)
        def _():
            y_copy(job, 2, second).start()
            y_copy(job, 0, first).wait_recv()
            first[...] = first[...] + y_in[job, 0, :quart_f, :]
            y_copy(job, 3, first).start()

        @pl.when(j == 2)
        def _():
            y_copy(job, 4, first).start()
            y_copy(job, 1, second).wait_recv()
            second[...] = second[...] + y_in[job, 0, quart_f:, :]
            y_copy(job, 5, second).start()

        @pl.when(j == 3)
        def _():
            for kind in range(2, 6):
                y_copy(job, kind, first).wait_recv()
            both[...] = both[...] + y_in[job, 1] + y_in[job, 2]

    def z_far(job, kind, src):
        dev = (to_z_up, to_z_down)[kind]
        return rcopy(src, z_hop.at[job], zs.at[job, kind], zh.at[job], dev)

    def z_near(job, place, kind, src):
        side, part, dev = ((1, lo, to_z_down), (1, hi, to_z_down), (0, hi, to_z_up), (0, lo, to_z_up))[kind]
        return rcopy(src, z_in.at[place, side, part], zs.at[job, kind % 2], zr.at[place, kind], dev)

    def z_first(job, place, rows, m, dist):
        first, second = rows(m, 0, quart_f), rows(m, quart_f, quart_f)

        @pl.when(dist == 2)
        def _():
            z_far(job, 0, first).start()
            z_far(job, 1, second).start()

        @pl.when(dist == 1)
        def _():
            z_near(job, place, 0, first).start()

        @pl.when(dist == 3)
        def _():
            z_near(job, place, 2, second).start()

    def z_middle(job, place, rows, m, dist):
        first, second = rows(m, 0, quart_f), rows(m, quart_f, quart_f)

        @pl.when(dist == 1)
        def _():
            z_far(job, 1, second).wait_recv()
            second[...] = second[...] + z_hop[job]
            z_near(job, place, 1, second).start()

        @pl.when(dist == 3)
        def _():
            z_far(job, 0, first).wait_recv()
            first[...] = first[...] + z_hop[job]
            z_near(job, place, 3, first).start()

    def z_root(job, place, rows, m):
        both = rows(m, 0, half_f)
        for kind in range(4):
            z_near(job, place, kind, rows(m, 0, quart_f)).wait_recv()
        both[...] = both[...] + z_in[place, 0] + z_in[place, 1]

    def dist_of(slot):
        block = jnp.where(slot == 0, h, jnp.where(slot == 1, h + 3, jnp.where(slot == 2, h + 1, h + 2)))
        return (z + 8 - block) % 4

    def place_of(m):
        slot = jnp.where(m < 12, m % 3, 3)
        return slot, jnp.where(m < 12, m // 3, m - 12), dist_of(slot)

    def when_mine(step, act):
        halves = jnp.where(step == split_at, core == 0, core == 1)
        mine = jnp.logical_and(
            jnp.logical_and(step >= 0, step <= split_at + 1),
            jnp.logical_or(step < split_at, halves),
        )

        @pl.when(mine)
        def _():
            m = jnp.where(step > split_at, split_at, step)
            act(m, *place_of(m))

    def stage_one(m, slot, j, dist):
        @pl.when(m < split_at)
        def _():
            core_copy(m).wait_recv()

        @pl.when(m == split_at)
        def _():
            last_core_copy(0).wait_recv()

        s = sums(m, 0, half_f)
        s[...] = s[...] + core_in[m % 4, :half_f, :]
        y_step(slot, sums, m, j)

        @pl.when(j == 3)
        def _():
            z_first(16 + slot, 4, sums, m, dist)

        @pl.when(m == split_at)
        def _():
            last_core_copy(1).wait_recv()

        s = upper(m)
        s[...] = s[...] + core_in[m % 4, half_f:, :]
        z_first(m, j, upper, m, dist)

    def stage_two(m, slot, j, dist):
        @pl.when(j == 3)
        def _():
            z_middle(16 + slot, 4, sums, m, dist)

        z_middle(m, j, upper, m, dist)

    def stage_three(m, slot, j, dist):
        @pl.when(dist == 0)
        def _():
            z_root(m, j, upper, m)
            y_step(4, upper, m, j)

            @pl.when(j == 3)
            def _():
                z_root(16 + slot, 4, sums, m)
                wq_ref[...] = sums(m)[...].T

    def times(rows):
        a_hi = gt_hi[rows, :]
        return mm(a_hi, x_hi[...]) + mm(a_hi, x_lo[...]) + mm(gt_lo[rows, :], x_hi[...])

    def tile_rows(ft, m=0):
        return pl.ds(pl.multiple_of(m * feats + ft * tile, tile), tile)

    def arrive(n):
        slot, j, _ = place_of(n)

        @pl.when(slot == 0)
        def _():
            pltpu.make_async_copy(x_cols(0), xbuf.at[n], own_sem.at[j]).wait()

        @pl.when(slot == 1)
        def _():
            rcopy(x_cols(0), xbuf.at[n], xs.at[0, j], xr.at[0, j], to_h_up).wait_recv()

            @pl.when(j < 3)
            def _():
                x_right2(j).start()

            @pl.when(j == 3)
            def _():
                x_right2(3, 0).start()
                x_right2(3, 1).start()

        @pl.when(slot == 2)
        def _():
            rcopy(x_cols(0), xbuf.at[n], xs.at[1, j], xr.at[1, j], to_h_down).wait_recv()

            @pl.when(j < 3)
            def _():
                x_left2(j).start()

            @pl.when(j == 3)
            def _():
                x_left2(3, 0).start()
                x_left2(3, 1).start()

        @pl.when(slot == 3)
        def _():
            x_right2(j).wait_recv()
            x_left2(j).wait_recv()

    def whole_unit(n):
        arrive(n)
        high, low = split(xbuf[n])
        x_hi[...] = high
        x_lo[...] = low

        @pl.when(n >= 4)
        def _():
            core_copy(n - 4).wait_send()

        def rows_of(ft, c2):
            acc = times(tile_rows(ft))
            left, right = acc[:, :128], acc[:, 128:]
            first = core == 0
            kv[tile_rows(ft, n), :] = jnp.where(first, left, right)
            gbuf[tile_rows(ft, n % 4), :] = jnp.where(first, right, left)
            return c2

        lax.fori_loop(0, feats // tile, rows_of, 0)
        core_copy(n).start()

    def half_unit(n):
        part = n - split_at

        @pl.when(part == 0)
        def _():
            x_right2(3, 0).wait_recv()
            x_left2(3, 0).wait_recv()
            core_copy(split_at - 4).wait_send()

        @pl.when(part == 1)
        def _():
            x_right2(3, 1).wait_recv()
            x_left2(3, 1).wait_recv()

        high, low = split(xbuf[split_at, :, pl.ds(pl.multiple_of(part * 128, 128), 128)])
        x_hi[:, :128] = high
        x_hi[:, 128:] = low

        def narrow(rows):
            both = mm(gt_hi[rows, :], x_hi[...])
            return both[:, :128] + both[:, 128:] + mm(gt_lo[rows, :], x_hi[:, :128])

        def kept(ft, c2):
            kv[tile_rows(ft, split_at), :] = narrow(tile_rows(ft))
            return c2

        def given(ft, c2):
            gbuf[tile_rows(ft, split_at % 4), :] = narrow(tile_rows(ft))

            @pl.when(ft == tiles // 2 - 1)
            def _():
                last_core_copy(0).start()

            return c2

        tiles = feats // tile

        @pl.when(core == part)
        def _():
            lax.fori_loop(0, tiles, kept, 0)

        @pl.when(core != part)
        def _():
            lax.fori_loop(0, tiles, given, 0)
            last_core_copy(1).start()

    def due(t, lag, late):
        m = jnp.where(jnp.logical_and(t >= lag, t < 12 + lag), t - lag, -1)
        for i, when in enumerate(late):
            m = jnp.where(t == when, 12 + i, m)
        return m

    def step(t, carry):
        n = due(t, 0, (17, 20, 23, 26, 29))

        @pl.when(jnp.logical_and(n >= 0, n < split_at))
        def _():
            whole_unit(n)

        @pl.when(n >= split_at)
        def _():
            half_unit(n)

        when_mine(due(t, 1, (18, 21, 24, 27, 30)), stage_one)
        when_mine(due(t, 3, (19, 22, 25, 28, 31)), stage_two)
        when_mine(due(t, 5, (20, 23, 26, 30, 32)), stage_three)
        return carry

    lax.fori_loop(0, 33, step, 0)

    out_copy.wait()
    for j in range(4):
        x_right(j).wait_send()
        x_left(j).wait_send()
    for j, part in ((0, None), (1, None), (2, None), (3, 0), (3, 1)):
        x_right2(j, part).wait_send()
        x_left2(j, part).wait_send()
    for p in range(1, 5):
        share(p).wait_send()
    for m in range(12, 15):
        core_copy(m).wait_send()
    last_core_copy(0).wait_send()
    last_core_copy(1).wait_send()

    def y_drain(job, carry):
        for kind in range(6):
            y_copy(job, kind, sums(0, 0, quart_f)).wait_send()
        return carry

    def z_drain(job, carry):
        slot, _, _ = place_of(job)
        slot = jnp.where(job < 16, slot, job - 16)

        @pl.when(dist_of(slot) != 0)
        def _():
            for kind in range(2):
                z_far(job, kind, sums(0, 0, quart_f)).wait_send()

        return carry

    lax.fori_loop(0, 5, y_drain, 0)
    lax.fori_loop(0, 20, z_drain, 0)


PIECES = 8


def hand_over(gq_in, wq_in, gq_out, wq_out, gq_buf, wq_buf, in_sem, out_sem):
    count = gq_buf.shape[0] // PIECES
    parts = [pl.ds(i * count, count) for i in range(PIECES)]
    fetch = [pltpu.make_async_copy(gq_in.at[p], gq_buf.at[p], in_sem.at[i]) for i, p in enumerate(parts)]
    store = [pltpu.make_async_copy(gq_buf.at[p], gq_out.at[p], out_sem.at[i]) for i, p in enumerate(parts)]
    fetch.append(pltpu.make_async_copy(wq_in, wq_buf, in_sem.at[PIECES]))
    store.append(pltpu.make_async_copy(wq_buf, wq_out, out_sem.at[PIECES]))
    for c in fetch:
        c.start()
    for f, c in zip(fetch, store):
        f.wait()
        c.start()
    for c in store:
        c.wait()


def body(tokens_x, keys, values, grad_out, level_table, level_bins):
    tokens, heads, hd = keys.shape
    feats = heads * hd
    used = (tokens * lax.axis_size("seq")).bit_length()
    quarter = tokens // 4
    dma = pltpu.SemaphoreType.DMA
    stack = max(tokens * heads * 2, 16 * feats)
    hbm = pl.BlockSpec(memory_space=pl.ANY)
    vmem = pl.BlockSpec(memory_space=pltpu.VMEM)
    gq, wq = pl.pallas_call(
        kernel,
        out_shape=(
            jax.ShapeDtypeStruct((tokens * heads, hd), F32),
            jax.ShapeDtypeStruct((128, feats), F32),
        ),
        in_specs=[hbm, hbm, hbm, hbm, vmem, vmem],
        out_specs=(hbm, vmem),
        scratch_shapes=[
            pltpu.VMEM((16, tokens, 256), F32),
            pltpu.VMEM((stack, hd), F32),
            pltpu.VMEM((max(tokens * heads, 4 * feats), hd), F32),
            pltpu.VMEM((tokens * heads, hd), F32),
            pltpu.VMEM((feats, tokens), BF16),
            pltpu.VMEM((feats, tokens), BF16),
            pltpu.VMEM((heads, used, tokens), F32),
            pltpu.VMEM((quarter, quarter), jnp.int32),
            pltpu.VMEM((heads, 4, hd, hd), F32),
            pltpu.VMEM((heads, hd, hd), F32),
            pltpu.VMEM((5, heads, hd, hd), F32),
            pltpu.VMEM((4, feats, 128), F32),
            pltpu.VMEM((5, 3, feats // 2, 128), F32),
            pltpu.VMEM((5, 2, feats // 2, 128), F32),
            pltpu.VMEM((20, feats // 4, 128), F32),
            pltpu.VMEM((tokens, 256), BF16),
            pltpu.VMEM((tokens, 256), BF16),
            dma((3,)),
            dma,
            dma((4,)),
            dma((4, 5)),
            dma((4, 5)),
            dma((5,)),
            dma((5,)),
            dma((5,)),
            dma((5,)),
            dma((17,)),
            dma((17,)),
            dma((5, 6)),
            dma((5, 6)),
            dma((20, 2)),
            dma((5, 4)),
            dma((20,)),
        ],
        compiler_params=pltpu.CompilerParams(
            collective_id=0, has_side_effects=True, vmem_limit_bytes=63 * 1024 * 1024,
        ),
        name="query_grad",
    )(
        tokens_x,
        keys.reshape(tokens * heads, hd),
        values.reshape(tokens * heads, hd),
        grad_out.reshape(tokens * heads, hd),
        level_table,
        level_bins.T,
    )
    rows = tokens * heads
    gq, wq = pl.pallas_call(
        hand_over,
        out_shape=(jax.ShapeDtypeStruct((rows, hd), F32), jax.ShapeDtypeStruct(wq.shape, F32)),
        in_specs=[hbm, hbm],
        out_specs=(hbm, hbm),
        scratch_shapes=[
            pltpu.VMEM((rows, hd), F32),
            pltpu.VMEM(wq.shape, F32),
            dma((PIECES + 1,)),
            dma((PIECES + 1,)),
        ],
        compiler_params=pltpu.CompilerParams(vmem_limit_bytes=62 * 1024 * 1024),
        name="hand_over",
    )(gq, wq)
    return gq.reshape(tokens, heads, hd), wq


def solution(mesh):
    in_specs = (
        P("seq", "head"),
        P("seq", "head", None),
        P("seq", "head", None),
        P("seq", "head", None),
        P("head", None, None),
        P("seq", "head"),
    )
    out_specs = (P("seq", "head", None), P("seq", "head"))
    return jax.shard_map(body, mesh=mesh, in_specs=in_specs, out_specs=out_specs, check_vma=False)
```
